128 devices in a mesh: seq: 8 (over x, core), cand: 16 (over y, z).
Axes of the slice: x: 4, y: 4, z: 4, core: 2. Of those that a mesh axis runs over, the one named last changes fastest.
Arguments:
- events: bfloat16 [16, 4096, 1024], P('cand', 'seq'), may hold values from -6 to 6
- lengths: int32 [16], P('cand'), may hold values from 1024 to 4096, as said below
- target_pos: int32 [16, 32], P('cand'), may hold values from 0 to 4095, as said below
- target_ids: int32 [16, 32], P('cand', 'seq'), may hold values from 0 to 524287
- items: bfloat16 [524288, 1024], P(('seq', 'cand')), may hold values from -0.1875 to 0.1875
- item_block: int32 [128], P(('seq', 'cand')), may hold values from 0 to 127, each once
- temper: float32 [16], replicated, may hold values from 1 to 64
- in_gain: float32 [1024], replicated, may hold values from 0.25 to 1.75
- w_xbc: bfloat16 [1024, 2304], replicated, may hold values from -0.1875 to 0.1875
- w_z: bfloat16 [1024, 2048], replicated, may hold values from -0.1875 to 0.1875
- w_dt: bfloat16 [1024, 32], replicated, may hold values from -0.1875 to 0.1875
- conv_w: float32 [4, 2304], replicated, may hold values from -3 to 3
- conv_b: float32 [2304], replicated, may hold values from -0.5 to 0.5
- dt_bias: float32 [32], replicated, may hold values from -8 to -3
- a_log: float32 [32], replicated, may hold values from -1.5 to 2.8
- d_skip: float32 [32], replicated, may hold values from 0.5 to 1.5
- norm_gain: float32 [2048], replicated, may hold values from 0.25 to 1.75
- w_out: bfloat16 [2048, 1024], replicated, may hold values from -0.125 to 0.125
- final_gain: float32 [1024], replicated, may hold values from 0.25 to 1.75
Outputs:
- layer_out: bfloat16 [16, 4096, 1024], P('cand', 'seq')
- loss: float32 [512], P(('seq', 'cand'))
The draws below stay inside these ranges and needn't reach their ends.
Inputs may be any that keep to these rules, and one draw needn't show every extreme that they name: `lengths`: one history in every draw has all 4096 events valid. `target_pos`: each target lies before its history's length.
All inputs are finite; a program needn't handle non-finite values.
Results may differ from the reference program's by a relative error of at most 0.0085.
Values may be sent and summed in bfloat16 or wider, within the bound.
No kernel may reach another device: no remote copies, remote signals or barrier semaphores. Data moves between devices by JAX's collectives and lax.ppermute only.
A program may use at most 128 MiB of HBM per device.

```python
import math
import jax
import jax.numpy as jnp
from jax import lax

D = 1024
E = 2048
H = 32
P_SIZE = 64
N = 128
K_CONV = 4
GROUP = 128
TGT_DEV = 4
ITEM_DEV = 4096
HLEN = 4096
HISTS = 16
TGT_HIST = 32
ITEMS = 524288
LOSS_ROWS = 512
N_SEQ = 8
DEVICES = 128


def history_pick(key):
    return jax.random.randint(jax.random.fold_in(key, 11), (), 0, HISTS)


def history_lengths(key):
    pick = history_pick(key)
    others = jax.random.randint(jax.random.fold_in(key, 12), (HISTS,), HLEN // 4, HLEN + 1)
    rows = jnp.arange(HISTS)
    shortest = (pick + 1) % HISTS
    others = jnp.where(rows == shortest, HLEN // 4, others)
    return jnp.where(rows == pick, HLEN, others).astype(jnp.int32)


def draw_lengths(key, part):
    return history_lengths(key)


def draw_target_pos(key, part):
    valid = history_lengths(key)
    pick = history_pick(key)
    key = jax.random.fold_in(key, 5)
    drawn = jax.random.randint(key, (HISTS, TGT_HIST), 0, valid[:, None])
    rows = jnp.arange(HISTS)[:, None]
    cols = jnp.arange(TGT_HIST)[None, :]
    drawn = jnp.where((rows == pick) & (cols == 0), HLEN - 1, drawn)
    drawn = jnp.where((rows == pick) & (cols == 1), 0, drawn)
    return drawn.astype(jnp.int32)


def draw_temper(key, part):
    key = jax.random.fold_in(key, 21)
    spread = jax.random.uniform(key, (HISTS,), jnp.float32, 0.0, math.log(8.0))
    drawn = jnp.exp(spread)
    return drawn.astype(jnp.float32)


def with_ends(array, rng, least, largest):
    spot = [jax.random.randint(jax.random.fold_in(rng, axis), (), 0, length) for axis, length in enumerate(array.shape)]
    main_axis = array.shape.index(max(array.shape))
    next_to = spot[:main_axis] + [(spot[main_axis] + 1) % array.shape[main_axis]] + spot[main_axis + 1:]
    return array.at[tuple(spot)].set(least).at[tuple(next_to)].set(largest)


def levels(rng, extent, pieces, smallest, top_value):
    level, own = 1.0, jax.random.fold_in(rng, 6)
    for dim, parts in pieces:
        draws = jnp.exp(jax.random.uniform(jax.random.fold_in(own, dim), (parts,), jnp.float32, smallest / len(pieces), top_value / len(pieces)))
        level = level * jnp.repeat(draws, extent[dim] // parts).reshape([-1 if axis == dim else 1 for axis in range(len(extent))])
    return level


def scatter_about(rng, shape, width, limit, split=(), kind=jnp.bfloat16):
    array = width * jax.random.normal(rng, shape, jnp.float32)
    if split:
        array = array * levels(rng, shape, split, -0.22, 0.18)
    return jnp.clip(array, -limit, limit).astype(kind)


def setup_inputs(seed: int = 0) -> dict:
    arg_keys = jax.random.split(jax.random.key(seed), 20)
    events = scatter_about(arg_keys[0], (HISTS, HLEN, D), 1.0, 6.0, ((0, 16), (1, 8)))
    lengths = draw_lengths(jax.random.fold_in(arg_keys[19], 71), 0)
    target_pos = draw_target_pos(jax.random.fold_in(arg_keys[19], 71), 0)
    target_ids = with_ends(jax.random.randint(arg_keys[3], (HISTS, TGT_HIST), 0, ITEMS), jax.random.fold_in(arg_keys[3], 1), 0, ITEMS - 1).astype(jnp.int32)
    items = scatter_about(arg_keys[4], (ITEMS, D), D ** -0.5, 0.1875, ((0, 128),))
    item_block = jax.random.permutation(arg_keys[5], DEVICES).astype(jnp.int32)
    temper = draw_temper(jax.random.fold_in(arg_keys[19], 71), 0)
    in_gain = jnp.clip(1.0 + 0.15 * jax.random.normal(arg_keys[7], (D,), jnp.float32), 0.25, 1.75)
    w_xbc = scatter_about(arg_keys[8], (D, E + 2 * N), D ** -0.5, 0.1875)
    w_z = scatter_about(arg_keys[9], (D, E), D ** -0.5, 0.1875)
    w_dt = scatter_about(arg_keys[10], (D, H), D ** -0.5, 0.1875)
    conv_w = scatter_about(arg_keys[11], (K_CONV, E + 2 * N), K_CONV ** -0.5, 3.0, (), jnp.float32)
    conv_b = jnp.clip(jax.random.uniform(arg_keys[12], (E + 2 * N,), jnp.float32, -0.5, 0.5), -0.5, 0.5)
    dt_bias = jnp.clip(jax.random.uniform(arg_keys[13], (H,), jnp.float32, -8.0, -3.0), -8.0, -3.0)
    a_log = jnp.clip(jax.random.uniform(arg_keys[14], (H,), jnp.float32, -1.5, 2.8), -1.5, 2.8)
    d_skip = jnp.clip(jax.random.uniform(arg_keys[15], (H,), jnp.float32, 0.5, 1.5), 0.5, 1.5)
    norm_gain = jnp.clip(1.0 + 0.15 * jax.random.normal(arg_keys[16], (E,), jnp.float32), 0.25, 1.75)
    w_out = scatter_about(arg_keys[17], (E, D), E ** -0.5, 0.125)
    final_gain = jnp.clip(1.0 + 0.15 * jax.random.normal(arg_keys[18], (D,), jnp.float32), 0.25, 1.75)
    return {"events": events, "lengths": lengths, "target_pos": target_pos, "target_ids": target_ids, "items": items, "item_block": item_block, "temper": temper, "in_gain": in_gain, "w_xbc": w_xbc, "w_z": w_z, "w_dt": w_dt, "conv_w": conv_w, "conv_b": conv_b, "dt_bias": dt_bias, "a_log": a_log, "d_skip": d_skip, "norm_gain": norm_gain, "w_out": w_out, "final_gain": final_gain}


EPS = 1e-05
HIGH = lax.Precision.HIGHEST

def rms(v, gain):
    return v * lax.rsqrt(lax.optimization_barrier(jnp.mean(v * v, axis=-1, keepdims=True)) + EPS) * gain

def layer(events_one, length, in_gain, w_xbc, w_z, w_dt, conv_w, conv_b, dt_bias, a_log, d_skip, norm_gain, w_out, final_gain):
    seq_len = events_one.shape[0]
    normed = rms(events_one.astype(jnp.float32), in_gain).astype(jnp.bfloat16)
    xbc_raw = jnp.dot(normed, w_xbc, preferred_element_type=jnp.float32).astype(jnp.bfloat16)
    gate_z = jnp.dot(normed, w_z, preferred_element_type=jnp.float32).astype(jnp.bfloat16)
    dt_raw = jnp.dot(normed, w_dt, preferred_element_type=jnp.float32)
    padded = jnp.concatenate([jnp.zeros((K_CONV - 1, xbc_raw.shape[1]), jnp.bfloat16), xbc_raw], axis=0).astype(jnp.float32)
    conv = conv_b
    for k in range(K_CONV):
        conv = conv + conv_w[k] * padded[k:k + seq_len]
    xbc = jax.nn.silu(conv)
    blocks = seq_len // GROUP
    xh = xbc[:, :E].reshape(blocks, GROUP, H, P_SIZE)
    bmat = xbc[:, E:E + N].reshape(blocks, GROUP, N)
    cmat = xbc[:, E + N:].reshape(blocks, GROUP, N)
    place = jnp.arange(seq_len, dtype=jnp.int32)
    valid = (place < length).astype(jnp.float32)
    step = jax.nn.softplus(dt_raw + dt_bias) * valid[:, None]
    logdec = (-step * jnp.exp(a_log)).reshape(blocks, GROUP, H)
    step = step.reshape(blocks, GROUP, H)
    cum = jnp.cumsum(logdec, axis=1)
    cum_t = jnp.transpose(cum, (0, 2, 1))
    diff = cum_t[:, :, :, None] - cum_t[:, :, None, :]
    rowi = jnp.arange(GROUP)[:, None]
    colj = jnp.arange(GROUP)[None, :]
    decay = jnp.exp(jnp.where((rowi >= colj)[None, None], diff, -jnp.inf))
    scores = jnp.einsum('cin,cjn->cij', cmat, bmat, precision=HIGH)
    weights = scores[:, None] * decay * jnp.transpose(step, (0, 2, 1))[:, :, None, :]
    y_in = jnp.einsum('chij,cjhp->cihp', weights, xh, precision=HIGH)
    tail = jnp.exp(cum[:, -1:, :] - cum) * step
    group_states = jnp.einsum('cjn,cjh,cjhp->chpn', bmat, tail, xh, precision=HIGH)
    group_decay = jnp.exp(cum[:, -1, :])

    def advance(state, inputs):
        g, s = inputs
        return (g[:, None, None] * state + s, state)
    zero_state = jnp.zeros((H, P_SIZE, N), jnp.float32)
    _, before = lax.scan(advance, zero_state, (group_decay, group_states))
    y_st = jnp.einsum('cin,chpn->cihp', cmat, before, precision=HIGH) * jnp.exp(cum)[..., None]
    y = (y_in + y_st + d_skip[:, None] * xh).reshape(seq_len, E)
    gated = y * jax.nn.silu(gate_z.astype(jnp.float32))
    mixed = rms(gated, norm_gain).astype(jnp.bfloat16)
    out = (events_one.astype(jnp.float32) + jnp.dot(mixed, w_out, preferred_element_type=jnp.float32)).astype(jnp.bfloat16)
    final = rms(out.astype(jnp.float32), final_gain).astype(jnp.bfloat16)
    return (out, final)

def reference(events, lengths, target_pos, target_ids, items, item_block, temper, in_gain, w_xbc, w_z, w_dt, conv_w, conv_b, dt_bias, a_log, d_skip, norm_gain, w_out, final_gain):

    def one(pair):
        return layer(pair[0], pair[1], in_gain, w_xbc, w_z, w_dt, conv_w, conv_b, dt_bias, a_log, d_skip, norm_gain, w_out, final_gain)
    layer_out, final = lax.map(one, (events, lengths))
    order_pos = jnp.transpose(target_pos.reshape(HISTS, N_SEQ, TGT_DEV), (1, 0, 2)).reshape(-1)
    order_ids = jnp.transpose(target_ids.reshape(HISTS, N_SEQ, TGT_DEV), (1, 0, 2)).reshape(-1)
    hist_of = jnp.broadcast_to(jnp.arange(HISTS, dtype=jnp.int32)[None, :, None], (N_SEQ, HISTS, TGT_DEV)).reshape(-1)
    rows = final[hist_of, order_pos]
    row_scale = temper[hist_of]
    table = items.reshape(DEVICES, ITEM_DEV, D)

    def online(carry, block):
        top, total = carry
        logit = row_scale[:, None] * lax.dot_general(rows, block, (((1,), (1,)), ((), ())), preferred_element_type=jnp.float32)
        new_top = jnp.maximum(top, lax.optimization_barrier(jnp.max(logit, axis=1)))
        total = total * jnp.exp(top - new_top) + lax.optimization_barrier(jnp.sum(jnp.exp(logit - new_top[:, None]), axis=1))
        return ((new_top, total), None)
    start = (jnp.full((LOSS_ROWS,), -1e+30, jnp.float32), jnp.zeros((LOSS_ROWS,), jnp.float32))
    (top, total), _ = lax.scan(online, start, table)
    inverse = jnp.zeros((DEVICES,), jnp.int32).at[item_block].set(jnp.arange(DEVICES, dtype=jnp.int32))
    row_index = inverse[order_ids // ITEM_DEV] * ITEM_DEV + order_ids % ITEM_DEV
    target_rows = items[row_index]
    target_logit = row_scale * lax.optimization_barrier(jnp.sum(rows.astype(jnp.float32) * target_rows.astype(jnp.float32), axis=1))
    loss = top + jnp.log(total) - target_logit
    return (layer_out, loss)
```

```python
import functools

import jax
import jax.numpy as jnp
from jax import lax
from jax.experimental import pallas as pl
from jax.experimental.pallas import tpu as pltpu
from jax.sharding import PartitionSpec as P

GROUP = 128
EPS = 1e-05
BLK = 256
HALO = 16
BF = jnp.bfloat16
F32 = jnp.float32
VMEM_LIMIT = 56 * 1024 * 1024


def rms(v, gain):
    return v * lax.rsqrt(jnp.mean(v * v, axis=-1, keepdims=True) + EPS) * gain


def silu(v):
    half = 0.5 * v
    return half + half * jnp.tanh(half)


def four(v):
    return jnp.concatenate([v, v, v, v], axis=1)


def lane_group(shape):
    return lax.broadcasted_iota(jnp.int32, shape, 1) // 32


def packed(v, parts):
    group = lane_group(v.shape)
    rest = v
    out = jnp.zeros_like(v)
    for part in range(parts):
        piece = rest.astype(BF).astype(F32)
        out = jnp.where(group == part, piece, out)
        rest = rest - piece
    return out.astype(BF)


def expander(first_head, heads, lanes, parts):
    shape = (128, heads * lanes)
    row = lax.broadcasted_iota(jnp.int32, shape, 0)
    col = lax.broadcasted_iota(jnp.int32, shape, 1)
    return ((row % 32 == first_head + col // lanes) & (row < 32 * parts)).astype(BF)


def dot(a, b):
    return jnp.dot(a, b, preferred_element_type=F32)


def dot_nt(a, b):
    return lax.dot_general(a, b, (((1,), (1,)), ((), ())), preferred_element_type=F32)


def gate_kernel(meta, ev, gain, w_z, w_dt, dt_bias, a_log, normed, z, cum_out, cum_t, packs):
    rows = ev.shape[0]

    @pl.when(pl.program_id(0) == 0)
    def _():
        normed[...] = rms(ev[...].astype(F32), gain[...]).astype(BF)
        raw = dot(normed[...], four(w_dt[...]))
        place = meta[0] * rows + lax.broadcasted_iota(jnp.int32, (rows, 128), 0)
        v = raw + four(dt_bias[...])
        soft = jnp.maximum(v, 0.0) + jnp.log1p(jnp.exp(-jnp.abs(v)))
        step = jnp.where(place < meta[1], soft, 0.0)
        logdec = -step * jnp.exp(four(a_log[...]))
        tri = (
            lax.broadcasted_iota(jnp.int32, (rows, rows), 0)
            >= lax.broadcasted_iota(jnp.int32, (rows, rows), 1)
        ).astype(BF)
        cum = dot(tri, packed(logdec, 3))
        cum = cum + pltpu.roll(cum, 32, 1)
        cum = cum + pltpu.roll(cum, 64, 1)
        cum_out[...] = packed(cum, 3)
        flipped = jnp.transpose(cum)
        for g in range(8):
            cum_t[g] = flipped[4 * g : 4 * g + 4]
        packs[0] = packed(step, 2)
        packs[1] = packed(jnp.exp(cum[rows - 1 :] - cum) * step, 2)
        packs[4] = packed(jnp.exp(cum), 2)
        for c in range(rows // GROUP):
            lo, hi = c * GROUP, (c + 1) * GROUP
            own = cum[lo:hi]
            packs[2, lo:hi] = packed(jnp.exp(cum[hi - 1 : hi] - own) * step[lo:hi], 2)
            start = cum[lo - 1 : lo] if c else 0.0
            packs[3, lo:hi] = packed(jnp.exp(own - start), 2)

    z[...] = dot(normed[...], w_z[...]).astype(BF)


def xbc_kernel(meta, normed, halo, gain, w, conv_w, conv_b, packs, x, bc, keep, send, full, raw, b_t):
    g = pl.program_id(0)
    rows = normed.shape[0]

    @pl.when(g == 0)
    def _():
        full[:HALO] = rms(halo[...].astype(F32), gain[...]).astype(BF)
        full[HALO:] = normed[...]

    raw[...] = dot(full[...], w[...]).astype(BF).astype(F32)
    conv = conv_b[...]
    for k in range(4):
        conv = conv + conv_w[k : k + 1] * raw[HALO - 3 + k : HALO - 3 + k + rows]
    act = silu(conv)

    @pl.when(g == 0)
    def _():
        bc[...] = act.astype(BF)
        b_t[...] = jnp.transpose(act[:, :128]).astype(BF)

    def state(out):
        blk = meta[3] ^ 4 if out is send else meta[3]
        first = (blk + (g - 1) % 4) * 4
        spread = expander(first, 4, 64, 2)
        weighted = (act * dot(packs[0], spread)).astype(BF)
        out[:128] = dot(b_t[...], weighted).astype(BF)
        whole = dot(packs[1, rows - 16 :], spread)
        out[128:] = jnp.broadcast_to(whole[15:], (16, BLK)).astype(BF)

    @pl.when(g > 0)
    def _():
        x[...] = act.astype(BF)

    @pl.when((g > 0) & (g < 5))
    def _():
        state(send)

    @pl.when(g >= 5)
    def _():
        state(keep)


def scan_kernel(x, bc, cum, cum_t, packs, d_skip, y, scores, b_t):
    g = pl.program_id(0)
    rows = x.shape[0]
    chunks = rows // GROUP

    @pl.when(g == 0)
    def _():
        lower = lax.broadcasted_iota(jnp.int32, (GROUP, GROUP), 0) >= lax.broadcasted_iota(
            jnp.int32, (GROUP, GROUP), 1
        )
        for c in range(chunks):
            part = slice(c * GROUP, (c + 1) * GROUP)
            scores[c] = jnp.where(lower, dot_nt(bc[part, 128:], bc[part, :128]), 0.0)
        b_t[...] = jnp.transpose(bc[:, :128].astype(F32)).astype(BF)

    spread = expander(4 * g, 4, 64, 2)
    wide = expander(4 * g, 4, GROUP, 3)
    skip = dot(packed(jnp.broadcast_to(four(d_skip[...]), (16, 128)), 2), spread)[:1]
    left = lax.broadcasted_iota(jnp.int32, (GROUP, 128), 1) < 64
    before = jnp.zeros((128, BLK), F32)
    for c in range(chunks):
        part = slice(c * GROUP, (c + 1) * GROUP)
        xc = x[part].astype(F32)
        stepped = xc * dot(packs[0, part], spread)
        tailed = (xc * dot(packs[2, part], spread)).astype(BF)
        inner = dot(packs[3, part], spread)
        own = dot(cum[part], wide)
        out = xc * skip
        if c:
            out = out + dot(bc[part, 128:], before.astype(BF)) * inner
        pairs = []
        for p in range(2):
            weights = []
            for h in (2 * p, 2 * p + 1):
                diff = own[:, h * GROUP : (h + 1) * GROUP] - cum_t[0, h : h + 1, part]
                weights.append((scores[c] * jnp.exp(jnp.minimum(diff, 0.0))).astype(BF))
            pair = stepped[:, p * 128 : (p + 1) * 128]
            stacked = jnp.concatenate(
                [jnp.where(left, pair, 0.0), jnp.where(left, 0.0, pair)], axis=0
            ).astype(BF)
            pairs.append(dot(jnp.concatenate(weights, axis=1), stacked))
        y[part] = (out + jnp.concatenate(pairs, axis=1)).astype(BF)
        if c < chunks - 1:
            before = before * inner[GROUP - 1 :] + dot(b_t[:, part], tailed)


def out_kernel(meta, y, bc, kept, got, packs, z, ev, norm_gain, w_out, final_gain, wanted, out, rows_out):
    i = pl.program_id(0)
    rows = y.shape[0]
    half = kept.shape[1]
    core = meta[2]
    mine, other = kept[...], got[...]
    entering = [jnp.where(core == 0, mine, other), jnp.where(core == 0, other, mine)]
    gated = []
    square = jnp.zeros((rows, 128), F32)
    for b in range(2 * half // BLK):
        cols = slice(b * BLK, (b + 1) * BLK)
        at = b * BLK % half
        e = entering[b * BLK // half][:128, at : at + BLK]
        add = dot(bc[:, 128:], e) * dot(packs[0], expander(4 * b, 4, 64, 2))
        v = (y[:, cols].astype(F32) + add) * silu(z[:, cols].astype(F32))
        sq = v * v
        square = square + sq[:, :128] + sq[:, 128:]
        gated.append(v)
    scale = lax.rsqrt(jnp.sum(square, axis=1, keepdims=True) * (1.0 / (2 * half)) + EPS)
    mixed = jnp.concatenate(
        [
            (gated[b] * scale * norm_gain[:, b * BLK : (b + 1) * BLK]).astype(BF)
            for b in range(2 * half // BLK)
        ],
        axis=1,
    )
    res = (ev[...].astype(F32) + dot(mixed, w_out[...])).astype(BF)
    out[...] = res
    final = rms(res.astype(F32), final_gain[...]).astype(BF)
    first = (meta[0] * pl.num_programs(0) + i) * rows
    place = first + lax.broadcasted_iota(jnp.int32, (32, rows), 1)
    pick = dot((place == wanted[...]).astype(BF), final)

    @pl.when(i == 0)
    def _():
        rows_out[...] = jnp.zeros_like(rows_out)

    for k in range(4):
        cols = slice(k * 1024, (k + 1) * 1024)
        rows_out[:, cols] = rows_out[:, cols] + pick[8 * k : 8 * k + 8]


def logit_kernel(meta, own, got, items, scale, stats, rows_all, ids, top, total, hit):
    step = pl.program_id(0)
    block = items.shape[0]
    count = own.shape[0]

    @pl.when(step == 0)
    def _():
        core = meta[2]
        for k in range(4):
            cols = slice(k * 1024, (k + 1) * 1024)
            mine, other = own[:, cols], got[:, cols]
            rows_all[2 * k * count : (2 * k + 1) * count] = jnp.where(core == 0, mine, other)
            rows_all[(2 * k + 1) * count : (2 * k + 2) * count] = jnp.where(core == 0, other, mine)
        mine, other = own[:, 4 * 1024 :].astype(F32), got[:, 4 * 1024 :].astype(F32)
        digits = jnp.concatenate(
            [jnp.where(core == 0, mine, other), jnp.where(core == 0, other, mine)], axis=0
        )
        digits = jnp.transpose(digits)
        lines = digits[:4] * 65536.0 + digits[4:8] * 256.0 + digits[8:12]
        for k in range(4):
            ids[:, k * 128 : (k + 1) * 128] = lines[k : k + 1].astype(jnp.int32)
        top[...] = jnp.full_like(top, -1e30)
        total[...] = jnp.zeros_like(total)
        hit[...] = jnp.zeros_like(hit)

    logit = dot_nt(items[...], rows_all[...]) * scale[...]
    place = lax.broadcasted_iota(jnp.int32, logit.shape, 0)
    at = ids[...] - (meta[4] * (pl.num_programs(0) * block) + step * block)
    hit[...] += jnp.sum(jnp.where(place == at, logit, 0.0), axis=0, keepdims=True)
    new = jnp.maximum(top[...], jnp.max(logit, axis=0, keepdims=True))
    total[...] = total[...] * jnp.exp(top[...] - new) + jnp.sum(
        jnp.exp(logit - new), axis=0, keepdims=True
    )
    top[...] = new

    @pl.when(step == pl.num_programs(0) - 1)
    def _():
        lines = [
            ref[:, k * 128 : (k + 1) * 128] for ref in (top, total, hit) for k in range(4)
        ]
        lines = jnp.concatenate(lines + [jnp.zeros((116, 128), F32)], axis=0)
        stats[...] = jnp.transpose(lines)[:, :16]


def call(kernel, grid, in_specs, out_specs, out_shape, scratch, flops, nbytes):
    return pl.pallas_call(
        kernel,
        grid_spec=pltpu.PrefetchScalarGridSpec(
            num_scalar_prefetch=1,
            grid=(grid,),
            in_specs=in_specs,
            out_specs=out_specs,
            scratch_shapes=scratch,
        ),
        out_shape=out_shape,
        compiler_params=pltpu.CompilerParams(vmem_limit_bytes=VMEM_LIMIT),
        cost_estimate=pl.CostEstimate(flops=flops, bytes_accessed=nbytes, transcendentals=0),
    )


def whole(*shape):
    return pl.BlockSpec(shape, lambda *_: (0,) * len(shape))


def joined(first, second):
    decay = second[128:129]
    return jnp.concatenate([first[:128] * decay + second[:128], first[128:] * second[128:]], axis=0)


def local(
    events, lengths, target_pos, target_ids, items, item_block, temper, in_gain, w_xbc, w_z, w_dt,
    conv_w, conv_b, dt_bias, a_log, d_skip, norm_gain, w_out, final_gain,
):
    rows, width = events.shape[1:]
    inner = w_z.shape[1]
    ev = events[0]
    x_at, core, seq = lax.axis_index("x"), lax.axis_index("core"), lax.axis_index(("x", "core"))
    meta = jnp.stack([seq, lengths[0], core, core * 4, item_block[0]]).astype(jnp.int32)
    order = ("core", "x", "cand")

    with jax.named_scope("halo"):
        halo = lax.ppermute(ev[rows - HALO :], ("x", "core"), [(i, i + 1) for i in range(7)])
    with jax.named_scope("ids"):
        digits = jnp.concatenate([target_ids // 65536, target_ids // 256 % 256, target_ids % 256], axis=1)
        digits = jnp.pad(digits, ((0, 0), (0, 116))).astype(BF)
        scale = jnp.broadcast_to(temper[None, :], (32, 16)).reshape(1, 512)

    with jax.named_scope("gate"):
        normed, z, cum, cum_t, packs = call(
            gate_kernel, 4,
            [
                whole(rows, width), whole(1, width),
                pl.BlockSpec((width, inner // 4), lambda g, m: (0, g)),
                whole(width, 32), whole(1, 32), whole(1, 32),
            ],
            [
                whole(rows, width), pl.BlockSpec((rows, inner // 4), lambda g, m: (0, g)),
                whole(rows, 128), whole(8, 4, rows), whole(5, rows, 128),
            ],
            [
                jax.ShapeDtypeStruct((rows, width), BF), jax.ShapeDtypeStruct((rows, inner), BF),
                jax.ShapeDtypeStruct((rows, 128), BF), jax.ShapeDtypeStruct((8, 4, rows), F32),
                jax.ShapeDtypeStruct((5, rows, 128), BF),
            ],
            [], 2 * rows * width * inner, 2 * width * inner + 8 * rows * inner,
        )(meta, ev, in_gain[None], w_z, w_dt, dt_bias[None], a_log[None])

    def column(g, m):
        return jnp.where(g == 0, 8, jnp.where(g < 5, (m[3] ^ 4) + g - 1, m[3] + g - 5))

    with jax.named_scope("xbc"):
        x, bc, keep, send = call(
            xbc_kernel, 9,
            [
                whole(rows, width), whole(HALO, width), whole(1, width),
                pl.BlockSpec((width, BLK), lambda g, m: (0, column(g, m))),
                pl.BlockSpec((4, BLK), lambda g, m: (0, column(g, m))),
                pl.BlockSpec((1, BLK), lambda g, m: (0, column(g, m))),
                whole(2, rows, 128),
            ],
            [
                pl.BlockSpec((rows, BLK), lambda g, m: (0, column(jnp.maximum(g, 1), m))),
                whole(rows, 256),
                pl.BlockSpec((144, BLK), lambda g, m: (0, jnp.maximum(g - 5, 0))),
                pl.BlockSpec((144, BLK), lambda g, m: (0, jnp.clip(g - 1, 0, 3))),
            ],
            [
                jax.ShapeDtypeStruct((rows, inner), BF), jax.ShapeDtypeStruct((rows, 256), BF),
                jax.ShapeDtypeStruct((144, inner // 2), BF), jax.ShapeDtypeStruct((144, inner // 2), BF),
            ],
            [
                pltpu.VMEM((rows + HALO, width), BF), pltpu.VMEM((rows + HALO, BLK), F32),
                pltpu.VMEM((128, rows), BF),
            ],
            2 * rows * width * 2304, 2 * width * 2304 + 4 * rows * inner,
        )(meta, normed, halo, in_gain[None], w_xbc, conv_w, conv_b[None], packs[jnp.array([1, 4])])

    swap = [(0, 1), (1, 0)]
    with jax.named_scope("states"):
        got = lax.ppermute(send, "core", swap).astype(F32)
        own = keep.astype(F32)
        first = jnp.where(core == 0, own, got)
        chip = joined(first, jnp.where(core == 0, got, own))
        near = lax.ppermute(chip.astype(BF), "x", [(0, 1), (1, 0), (2, 3), (3, 2)]).astype(F32)
        odd = x_at % 2 == 1
        pair = joined(jnp.where(odd, near, chip), jnp.where(odd, chip, near))
        far = lax.ppermute(pair.astype(BF), "x", [(1, 2), (0, 3)]).astype(F32)[:128]
        enter = jnp.where(odd, near[:128] + near[128:129] * far, far)
        later = first[:128] + first[128:129] * enter
        here = jnp.where(core == 0, enter, later).astype(BF)
        there = lax.ppermute(jnp.where(core == 0, later, enter).astype(BF), "core", swap)

    with jax.named_scope("scan"):
        y = call(
            scan_kernel_meta, inner // BLK,
            [
                pl.BlockSpec((rows, BLK), lambda g, m: (0, g)), whole(rows, 256), whole(rows, 128),
                pl.BlockSpec((1, 4, rows), lambda g, m: (g, 0, 0)), whole(5, rows, 128), whole(1, 32),
            ],
            pl.BlockSpec((rows, BLK), lambda g, m: (0, g)),
            jax.ShapeDtypeStruct((rows, inner), BF),
            [pltpu.VMEM((rows // GROUP, GROUP, GROUP), F32), pltpu.VMEM((128, rows), BF)],
            8 * rows * 128 * inner, 4 * rows * inner,
        )(meta, x, bc, cum, cum_t, packs, d_skip[None])

    part = 128
    with jax.named_scope("out"):
        out, picked = call(
            out_kernel, rows // part,
            [
                pl.BlockSpec((part, inner), lambda i, m: (i, 0)),
                pl.BlockSpec((part, 256), lambda i, m: (i, 0)),
                whole(128, inner // 2), whole(128, inner // 2),
                pl.BlockSpec((1, part, 128), lambda i, m: (4, i, 0)),
                pl.BlockSpec((part, inner), lambda i, m: (i, 0)),
                pl.BlockSpec((part, width), lambda i, m: (i, 0)),
                whole(1, inner), whole(inner, width), whole(1, width), whole(32, 1),
            ],
            [pl.BlockSpec((part, width), lambda i, m: (i, 0)), whole(8, 4 * width)],
            [jax.ShapeDtypeStruct((rows, width), BF), jax.ShapeDtypeStruct((8, 4 * width), F32)],
            [], 2 * rows * inner * (width + 128), 2 * inner * width + 6 * rows * inner,
        )(
            meta, y, bc, here, there, packs, z, ev, norm_gain[None], w_out, final_gain[None],
            jnp.transpose(target_pos.reshape(8, 4)).reshape(32, 1),
        )

    with jax.named_scope("rows"):
        mine = lax.all_to_all(picked.astype(BF), ("x", "core"), 0, 0, tiled=True)
        mine = jnp.sum(mine.astype(F32), axis=0, keepdims=True).astype(BF)
        mine = jnp.concatenate([mine, digits], axis=1)
        own_rows = lax.all_to_all(
            jnp.broadcast_to(mine, (64, mine.shape[1])), ("x", "cand"), 0, 0, tiled=True
        )
        got_rows = lax.ppermute(own_rows, "core", swap)

    steps = 8
    block = items.shape[0] // steps
    with jax.named_scope("logits"):
        stats = call(
            logit_kernel, steps,
            [
                whole(64, 4 * width + 128), whole(64, 4 * width + 128),
                pl.BlockSpec((block, width), lambda g, m: (g, 0)), whole(1, 512),
            ],
            whole(128, 16),
            jax.ShapeDtypeStruct((128, 16), F32),
            [pltpu.VMEM((512, width), BF), pltpu.VMEM((1, 512), jnp.int32)]
            + [pltpu.VMEM((1, 512), F32)] * 3,
            2 * 512 * items.shape[0] * width, 2 * items.shape[0] * width,
        )(meta, own_rows, got_rows, items, scale)

    with jax.named_scope("loss"):
        seen = lax.all_to_all(stats, order, 0, 0, tiled=True)
        top, total, hit = seen[:, 0:4], seen[:, 4:8], seen[:, 8:12]
        peak = jnp.max(top, axis=0)
        loss = peak + jnp.log(jnp.sum(total * jnp.exp(top - peak), axis=0)) - jnp.sum(hit, axis=0)
    return (out[None], loss)


def scan_kernel_meta(meta, *refs):
    scan_kernel(*refs)


def solution(mesh):
    fine = jax.sharding.Mesh(
        mesh.devices.reshape(mesh.shape["seq"] // 2, 2, mesh.shape["cand"]), ("x", "core", "cand")
    )
    seq = ("x", "core")
    each = ("x", "core", "cand")
    placed = (
        P("cand", seq, None),
        P("cand"),
        P("cand", None),
        P("cand", seq),
        P(each, None),
        P(each),
    ) + (P(),) * 13
    return jax.shard_map(
        local,
        mesh=fine,
        in_specs=placed,
        out_specs=(P("cand", seq, None), P(each)),
        check_vma=False,
    )
```

```python
import jax
import jax.numpy as jnp
import numpy as np
from jax import lax
from jax.experimental import pallas as pl
from jax.experimental.pallas import tpu as pltpu
from jax.sharding import PartitionSpec as P

GROUP = 128
EPS = 1e-05
BLK = 256
HALO = 16
PART = 64
BF = jnp.bfloat16
F32 = jnp.float32
SEQ = ("x", "core")
EACH = ("core", "x", "cand")
VMEM = pl.BlockSpec(memory_space=pltpu.VMEM)
HBM = pl.BlockSpec(memory_space=pl.ANY)
SMEM = pl.BlockSpec(memory_space=pltpu.SMEM)


def rms(v, gain):
    return v * lax.rsqrt(jnp.mean(v * v, axis=-1, keepdims=True) + EPS) * gain


def silu(v):
    half = 0.5 * v
    return half + half * jnp.tanh(half)


def four(v, axis=1):
    return jnp.concatenate([v, v, v, v], axis=axis)


def packed(v, parts):
    group = lax.broadcasted_iota(jnp.int32, v.shape, 1) // 32
    rest = v
    out = jnp.zeros_like(v)
    for part in range(parts):
        piece = rest.astype(BF).astype(F32)
        out = jnp.where(group == part, piece, out)
        rest = rest - piece
    return out.astype(BF)


def expander(heads, lanes, parts):
    row = np.arange(128)[:, None]
    col = np.arange(heads * lanes)[None, :]
    return jnp.asarray((row % 32 == col // lanes) & (row < 32 * parts), BF)


def dot(a, b):
    return jnp.dot(a, b, preferred_element_type=F32)


def dot_nt(a, b):
    return lax.dot_general(a, b, (((1,), (1,)), ((), ())), preferred_element_type=F32)


def blocks(total, size):
    return [slice(i, i + size) for i in range(0, total, size)]


def call(kernel, out_shape, specs, scratch=(), flops=0, limit=12, outs=None):
    many = isinstance(out_shape, (list, tuple))
    return pl.pallas_call(
        kernel,
        in_specs=specs,
        out_specs=outs or ([VMEM] * len(out_shape) if many else VMEM),
        out_shape=out_shape,
        scratch_shapes=list(scratch),
        compiler_params=pltpu.CompilerParams(vmem_limit_bytes=limit * 1024 * 1024),
        cost_estimate=pl.CostEstimate(flops=flops, bytes_accessed=0, transcendentals=0),
    )


def shape(*dims, dtype=BF):
    return jax.ShapeDtypeStruct(dims, dtype)


def fetches(pairs, sems, started=None):
    copies = [pltpu.make_async_copy(src, dst, sems.at[i]) for i, (src, dst) in enumerate(pairs)]
    for copy in copies[:started]:
        copy.start()
    return copies


def mix_kernel(
    length, ev_h, gain_h, w_dt_h, dt_bias_h, a_log_h, halo_h, w_h, conv_w_h, conv_b_h, spread_h,
    normed_h, cum_out, cum_t, shard, chunk, x_h, bc, keep, send,
    ev, gain, w_dt, dt_bias, a_log, halo, w, conv_w, conv_b, spread,
    full, x, raw, tail, weighted, b_t, states, sems, out_sems,
):
    rows, inner = x.shape
    order = [slice(inner, inner + BLK)] + blocks(inner, BLK)
    copies = fetches(
        [
            (ev_h, ev), (gain_h, gain), (w_dt_h, w_dt), (dt_bias_h, dt_bias), (a_log_h, a_log),
            (halo_h, halo), (conv_w_h, conv_w), (conv_b_h, conv_b), (spread_h, spread), (w_h, w),
        ],
        sems,
    )
    for copy in copies[:6]:
        copy.wait()
    full[:HALO] = rms(halo[...].astype(F32), gain[...]).astype(BF)
    for part in blocks(rows, PART):
        full[HALO + part.start : HALO + part.stop] = rms(ev[part].astype(F32), gain[...]).astype(BF)
    pre = dot_nt(full[HALO:], four(w_dt[...], 0))
    place = lax.axis_index(SEQ) * rows + lax.broadcasted_iota(jnp.int32, (rows, 128), 0)
    v = pre + four(dt_bias[...])
    soft = jnp.maximum(v, 0.0) + jnp.log1p(jnp.exp(-jnp.abs(v)))
    step = jnp.where(place < length[0], soft, 0.0)
    logdec = -step * jnp.exp(four(a_log[...]))
    lower = (
        lax.broadcasted_iota(jnp.int32, (rows, rows), 0)
        >= lax.broadcasted_iota(jnp.int32, (rows, rows), 1)
    ).astype(BF)
    cum = dot(lower, packed(logdec, 3))
    cum = cum + pltpu.roll(cum, 32, 1)
    cum = cum + pltpu.roll(cum, 64, 1)
    cum_out[...] = packed(cum, 3)
    flipped = jnp.transpose(cum)
    for g in range(8):
        cum_t[g] = flipped[4 * g : 4 * g + 4]
    shard[0] = packed(jnp.exp(cum[rows - 1 :] - cum) * step, 2)
    shard[1] = packed(jnp.exp(cum), 2)
    chunk[0] = packed(step, 2)
    for c, part in enumerate(blocks(rows, GROUP)):
        own = cum[part]
        chunk[1, part] = packed(jnp.exp(own[GROUP - 1 :] - own) * step[part], 2)
        chunk[2, part] = packed(jnp.exp(own - (cum[part.start - 1 : part.start] if c else 0.0)), 2)
    for copy in copies[6:]:
        copy.wait()
    stores = [pltpu.make_async_copy(full.at[HALO:], normed_h, out_sems.at[8])]
    stores[0].start()
    for n, cols in enumerate(order):
        slot = n % 2
        both = dot(full[...], w[:, cols])
        raw[slot, 0] = both[:, :128]
        raw[slot, 1] = both[:, 128:]
        if n:
            tail[slot] = dot(shard[0], spread[:, cols])
        for j in range(2):
            at = cols.start // 128 + j
            lanes = slice(at * 128, (at + 1) * 128)
            local_lanes = slice(j * 128, (j + 1) * 128)
            for part in blocks(rows, PART):
                conv = conv_b[at : at + 1]
                for k in range(4):
                    first = HALO - 3 + k + part.start
                    conv = conv + conv_w[k : k + 1, lanes] * raw[slot, j, first : first + PART]
                act = silu(conv)
                if n:
                    x[part, lanes] = act.astype(BF)
                    weighted[slot, part, local_lanes] = (act * tail[slot, part, local_lanes]).astype(BF)
                else:
                    bc[part, local_lanes] = act.astype(BF)
        if n:
            stores += fetches([(x.at[:, cols], x_h.at[:, cols])], out_sems.at[n - 1 : n])
            states[:128, cols] = dot(b_t[...], weighted[slot]).astype(BF)
            decay = dot(shard[1, rows - 16 :], spread[:, cols])
            states[128:, cols] = jnp.broadcast_to(decay[15:], (16, BLK)).astype(BF)
        else:
            b_t[...] = jnp.transpose(bc[:, :128].astype(F32)).astype(BF)
    first = lax.axis_index("core") == 0
    half = inner // 2
    for part in blocks(144, 48):
        low, high = states[part, :half], states[part, half:]
        keep[part] = jnp.where(first, low, high)
        send[part] = jnp.where(first, high, low)
    for store in stores:
        store.wait()


def join(first, second, out):
    decay = second[128:129].astype(F32)
    for part in blocks(128, PART):
        out[part] = (first[part].astype(F32) * decay + second[part].astype(F32)).astype(BF)
    out[128:] = (first[128:].astype(F32) * second[128:].astype(F32)).astype(BF)


def chip_kernel(keep, got, chip):
    @pl.when(lax.axis_index("core") == 0)
    def _():
        join(keep, got, chip)

    @pl.when(lax.axis_index("core") == 1)
    def _():
        join(got, keep, chip)


def pair_kernel(chip, near, pair):
    odd = lax.axis_index("x") % 2

    @pl.when(odd == 1)
    def _():
        join(near, chip, pair)

    @pl.when(odd == 0)
    def _():
        join(chip, near, pair)


def enter_kernel(keep, got, near, far, here, away):
    odd = (lax.axis_index("x") % 2 == 1).astype(F32)
    front = lax.axis_index("core") == 0
    near_decay = near[128:129].astype(F32) * odd + (1.0 - odd)
    decay = jnp.where(front, keep[128:129].astype(F32), got[128:129].astype(F32))
    for part in blocks(128, PART):
        enter = near[part].astype(F32) * odd + near_decay * far[part].astype(F32)
        first = jnp.where(front, keep[part].astype(F32), got[part].astype(F32))
        later = first + decay * enter
        here[part] = jnp.where(front, enter, later).astype(BF)
        away[part] = jnp.where(front, later, enter).astype(BF)


def scan_kernel(lo, hi, x, bc, cum, cum_t, chunk, spread, wide, d_skip, y, scores, b_t, lines):
    rows = x.shape[0]
    lower = lax.broadcasted_iota(jnp.int32, (GROUP, GROUP), 0) >= lax.broadcasted_iota(
        jnp.int32, (GROUP, GROUP), 1
    )
    for c, part in enumerate(blocks(rows, GROUP)):
        scores[c] = jnp.where(lower, dot_nt(bc[part, 128:], bc[part, :128]), 0.0)
    b_t[...] = jnp.transpose(bc[:, :128].astype(F32)).astype(BF)
    lines[...] = packed(jnp.broadcast_to(four(d_skip[...]), (16, 128)), 2)
    left = lax.broadcasted_iota(jnp.int32, (GROUP, 128), 1) < 64

    def group(g, _):
        cols = pl.ds(pl.multiple_of(g * BLK, BLK), BLK)
        to = pl.ds(pl.multiple_of((g - lo) * BLK, BLK), BLK)
        sp = spread[:, cols]
        wd = wide[:, pl.ds(pl.multiple_of(g * 4 * GROUP, 4 * GROUP), 4 * GROUP)]
        skip = dot(lines[...], sp)[:1]
        before = jnp.zeros((128, BLK), F32)
        for c, part in enumerate(blocks(rows, GROUP)):
            xc = x[part, cols].astype(F32)
            stepped = xc * dot(chunk[0, part], sp)
            inside = dot(chunk[2, part], sp)
            own = dot(cum[part], wd)
            out = xc * skip
            if c:
                out = out + dot(bc[part, 128:], before.astype(BF)) * inside
            pairs = []
            for p in range(2):
                weights = []
                for h in (2 * p, 2 * p + 1):
                    diff = own[:, h * GROUP : (h + 1) * GROUP] - cum_t[g, h : h + 1, part]
                    weights.append((scores[c] * jnp.exp(jnp.minimum(diff, 0.0))).astype(BF))
                pair = stepped[:, p * 128 : (p + 1) * 128]
                stacked = jnp.concatenate(
                    [jnp.where(left, pair, 0.0), jnp.where(left, 0.0, pair)], axis=0
                ).astype(BF)
                pairs.append(dot(jnp.concatenate(weights, axis=1), stacked))
            y[part, to] = (out + jnp.concatenate(pairs, axis=1)).astype(BF)
            if c < rows // GROUP - 1:
                tailed = (xc * dot(chunk[1, part], sp)).astype(BF)
                before = before * inside[GROUP - 1 :] + dot(b_t[:, part], tailed)
        return 0

    lax.fori_loop(lo, hi, group, 0)


def out_kernel(
    y_a, y_b, bc, kept, got, shard, z, ev, norm_gain, w_out, final_gain, wanted, spread,
    out, picked, mixed, square, enter, total, final,
):
    rows, inner = z.shape
    split = y_a.shape[1]
    width = ev.shape[1]
    half = inner // 2
    first = lax.axis_index("core") == 0
    enter[:, :half] = jnp.where(first, kept[...], got[...])
    enter[:, half:] = jnp.where(first, got[...], kept[...])
    for n, cols in enumerate(blocks(inner, BLK)):
        state = dot(bc[:, 128:], enter[:, cols])
        decay = dot(shard[1], spread[:, cols])
        for part in blocks(rows, PART):
            y = y_a[part, cols] if cols.stop <= split else y_b[part, cols.start - split : cols.stop - split]
            v = y.astype(F32) + state[part] * decay[part]
            v = v * silu(z[part, cols].astype(F32))
            sq = v * v
            sq = sq[:, :128] + sq[:, 128:]
            square[part] = square[part] + sq if n else sq
            mixed[part, cols] = (v * norm_gain[:, cols]).astype(BF)
    for cols in blocks(width, BLK):
        total[:, cols] = dot(mixed[...], w_out[:, cols])
    for part in blocks(rows, PART):
        mean = jnp.sum(square[part], axis=1, keepdims=True) * (1.0 / inner)
        res = (ev[part].astype(F32) + total[part] * lax.rsqrt(mean + EPS)).astype(BF)
        out[part] = res
        final[part] = rms(res.astype(F32), final_gain[...]).astype(BF)
    place = lax.axis_index(SEQ) * rows + lax.broadcasted_iota(jnp.int32, (32, rows), 1)
    column = jnp.transpose(jnp.broadcast_to(wanted[...].astype(F32), (128, 32)))[:, :1]
    pick = dot((place.astype(F32) == column).astype(BF), final[...]).astype(BF)
    for s in range(8):
        picked[s] = pick[4 * s : 4 * s + 4]


def rows_kernel(ids, got, sent):
    width = got.shape[2]
    mine = got[0].astype(F32)
    for s in range(1, got.shape[0]):
        mine = mine + got[s].astype(F32)
    row = lax.broadcasted_iota(jnp.int32, (4, 128), 0)
    lane = lax.broadcasted_iota(jnp.int32, (4, 128), 1)
    own = jnp.zeros((4, 128), jnp.int32)
    for k in range(4):
        own = jnp.where(row == k, ids[0, k], own)
    digits = jnp.where(lane == 0, own >> 16, jnp.where(lane == 1, (own >> 8) & 255, own & 255))
    digits = jnp.where(lane < 3, digits, 0).astype(F32)
    both = jnp.concatenate([mine, digits], axis=1).astype(BF)
    count = sent.shape[0] // 2
    for d in range(count):
        sent[d] = both[:2]
        sent[count + d] = both[2:]


def logit_kernel(block_id, temper, own, got, items, stats, rows, ids, scale):
    count, width = own.shape[0], items.shape[1]
    first = lax.axis_index("core") == 0
    for part in blocks(count, PART):
        mine, other = own[part], got[part]
        low = jnp.where(first, mine, other)
        high = jnp.where(first, other, mine)
        rows[part] = low[:, :width]
        rows[count + part.start : count + part.stop] = high[:, :width]
    for n in range(2):
        digits = jnp.where(first == (n == 0), own[:, width:], got[:, width:]).astype(F32)
        digits = jnp.transpose(digits)
        value = digits[0:1] * 65536.0 + digits[1:2] * 256.0 + digits[2:3]
        ids[:, n * count : (n + 1) * count] = value.astype(jnp.int32)
    history = lax.broadcasted_iota(jnp.int32, scale.shape, 1) // 2 % 16
    factor = jnp.zeros(scale.shape, F32)
    for c in range(16):
        factor = jnp.where(history == c, temper[c], factor)
    scale[...] = factor
    top = jnp.full(scale.shape, -1e30, F32)
    total = jnp.zeros(scale.shape, F32)
    hit = jnp.zeros(scale.shape, F32)
    base = ids[...] - block_id[0] * items.shape[0]
    for part in blocks(items.shape[0], 512):
        logit = dot_nt(items[part], rows[...]) * scale[...]
        place = lax.broadcasted_iota(jnp.int32, logit.shape, 0)
        hit = hit + jnp.sum(jnp.where(place == base - part.start, logit, 0.0), axis=0, keepdims=True)
        new = jnp.maximum(top, jnp.max(logit, axis=0, keepdims=True))
        total = total * jnp.exp(top - new) + jnp.sum(jnp.exp(logit - new), axis=0, keepdims=True)
        top = new
    gap = jnp.zeros((5, count), F32)
    lines = []
    for n in range(2):
        lines += [v[:, n * count : (n + 1) * count] for v in (top, total, hit)] + [gap]
    lines = jnp.concatenate(lines + [jnp.zeros((112, count), F32)], axis=0)
    stats[...] = jnp.transpose(lines)[:, :16]


def local(
    events, lengths, target_pos, target_ids, items, item_block, temper, in_gain, w_xbc, w_z, w_dt,
    conv_w, conv_b, dt_bias, a_log, d_skip, norm_gain, w_out, final_gain,
):
    rows, width = events.shape[1:]
    inner = w_z.shape[1]
    ev = events[0]
    spread = expander(32, 64, 2)
    wide = expander(32, GROUP, 3)
    chunks = rows // GROUP

    with jax.named_scope("halo"):
        halo = lax.ppermute(ev[rows - HALO :], SEQ, [(i, i + 1) for i in range(7)])

    with jax.named_scope("mix"):
        normed, cum, cum_t, shard, chunk, x, bc, keep, send = call(
            mix_kernel,
            [
                shape(rows, width), shape(rows, 128), shape(8, 4, rows, dtype=F32),
                shape(2, rows, 128), shape(3, rows, 128), shape(rows, inner), shape(rows, 256),
                shape(144, inner // 2), shape(144, inner // 2),
            ],
            [SMEM] + [HBM] * 10,
            [
                pltpu.VMEM((rows, width), BF), pltpu.VMEM((1, width), F32), pltpu.VMEM((32, width), BF),
                pltpu.VMEM((1, 32), F32), pltpu.VMEM((1, 32), F32), pltpu.VMEM((HALO, width), BF),
                pltpu.VMEM(w_xbc.shape, BF), pltpu.VMEM(conv_w.shape, F32),
                pltpu.VMEM((conv_b.shape[0] // 128, 128), F32), pltpu.VMEM(spread.shape, BF),
                pltpu.VMEM((rows + HALO, width), BF), pltpu.VMEM((rows, inner), BF),
                pltpu.VMEM((2, 2, rows + HALO, 128), F32),
                pltpu.VMEM((2, rows, BLK), F32), pltpu.VMEM((2, rows, BLK), BF),
                pltpu.VMEM((128, rows), BF), pltpu.VMEM((144, inner), BF),
                pltpu.SemaphoreType.DMA((10,)), pltpu.SemaphoreType.DMA((9,)),
            ],
            2 * rows * width * 2304,
            limit=56,
            outs=[HBM] + [VMEM] * 4 + [HBM] + [VMEM] * 3,
        )(
            lengths, ev, in_gain[None], w_dt.T, dt_bias[None], a_log[None], halo, w_xbc, conv_w,
            conv_b.reshape(-1, 128), spread,
        )

    def scan(lo, hi, x):
        return call(
            lambda *refs: scan_kernel(lo, hi, *refs),
            shape(rows, (hi - lo) * BLK),
            [VMEM] * 8,
            [
                pltpu.VMEM((chunks, GROUP, GROUP), F32), pltpu.VMEM((128, rows), BF),
                pltpu.VMEM((16, 128), BF),
            ],
            16 * rows * 128 * (hi - lo) * BLK,
        )(x, bc, cum, cum_t, chunk, spread, wide, d_skip[None])

    swap = [(0, 1), (1, 0)]
    payload = shape(144, inner // 2)
    entry = shape(128, inner // 2)
    with jax.named_scope("chip"):
        got = lax.ppermute(send, "core", swap)
        chip = call(chip_kernel, payload, [VMEM] * 2)(keep, got)
        sent, x = lax.optimization_barrier((chip, x))
        near = lax.ppermute(sent, "x", [(0, 1), (1, 0), (2, 3), (3, 2)])
    with jax.named_scope("scan"):
        y_a = scan(0, 5, x)
    with jax.named_scope("pair"):
        pair = call(pair_kernel, payload, [VMEM] * 2)(chip, near)
        sent, y_a, x, source = lax.optimization_barrier((pair, y_a, x, normed))
        far = lax.ppermute(sent, "x", [(1, 2), (0, 3)])
    with jax.named_scope("gate"):
        z = dot(source, w_z).astype(BF)
    with jax.named_scope("scan"):
        y_b = scan(5, 8, x)
    with jax.named_scope("enter"):
        here, away = call(enter_kernel, [entry, entry], [VMEM] * 4)(keep, got, near, far)
        away, z, y_b = lax.optimization_barrier((away, z, y_b))
        there = lax.ppermute(away, "core", swap)

    with jax.named_scope("out"):
        out, picked = call(
            out_kernel,
            [shape(rows, width), shape(8, 4, width)],
            [VMEM] * 13,
            [
                pltpu.VMEM((rows, inner), BF), pltpu.VMEM((rows, 128), F32), pltpu.VMEM((128, inner), BF),
                pltpu.VMEM((rows, width), F32), pltpu.VMEM((rows, width), BF),
            ],
            2 * rows * inner * (width + 256),
            limit=14,
        )(
            y_a, y_b, bc, here, there, shard, z, ev, norm_gain[None], w_out, final_gain[None], target_pos,
            spread,
        )

    with jax.named_scope("rows"):
        mine = lax.all_to_all(picked, SEQ, 0, 0, tiled=True)
        sent = call(rows_kernel, shape(128, 2, width + 128), [SMEM, VMEM], flops=10**10)(target_ids, mine)
        own_rows = lax.all_to_all(sent, EACH, 0, 0, tiled=True).reshape(256, width + 128)
        got_rows = lax.ppermute(own_rows, "core", swap)

    with jax.named_scope("logits"):
        stats = call(
            logit_kernel,
            shape(256, 16, dtype=F32),
            [SMEM, SMEM, VMEM, VMEM, VMEM],
            [
                pltpu.VMEM((512, width), BF), pltpu.VMEM((1, 512), jnp.int32), pltpu.VMEM((1, 512), F32),
            ],
            2 * 512 * items.shape[0] * width,
        )(item_block, temper, own_rows, got_rows, items)

    with jax.named_scope("loss"):
        seen = lax.all_to_all(stats.reshape(128, 2, 16), EACH, 0, 0, tiled=True)
        top, total, hit = [
            jnp.concatenate([seen[:, :, n], seen[:, :, n + 8]], axis=1) for n in range(3)
        ]
        peak = jnp.max(top, axis=0)
        loss = peak + jnp.log(jnp.sum(total * jnp.exp(top - peak), axis=0)) - jnp.sum(hit, axis=0)
    return (out[None], loss)


def solution(mesh):
    fine = jax.sharding.Mesh(
        mesh.devices.reshape(mesh.shape["seq"] // 2, 2, mesh.shape["cand"]), ("x", "core", "cand")
    )
    each = ("x", "core", "cand")
    placed = (
        P("cand", SEQ, None),
        P("cand"),
        P("cand", None),
        P("cand", SEQ),
        P(each, None),
        P(each),
    ) + (P(),) * 13
    return jax.shard_map(
        local,
        mesh=fine,
        in_specs=placed,
        out_specs=(P("cand", SEQ, None), P(each)),
        check_vma=False,
    )
```

```python
import jax
import jax.numpy as jnp
import numpy as np
from jax import lax
from jax.experimental import pallas as pl
from jax.experimental.pallas import tpu as pltpu
from jax.sharding import PartitionSpec as P

GROUP = 128
EPS = 1e-05
BLK = 256
HALO = 16
PART = 64
BF = jnp.bfloat16
F32 = jnp.float32
SEQ = ("x", "core")
EACH = ("core", "x", "cand")
VMEM = pl.BlockSpec(memory_space=pltpu.VMEM)
HBM = pl.BlockSpec(memory_space=pl.ANY)
SMEM = pl.BlockSpec(memory_space=pltpu.SMEM)


def rms(v, gain):
    return v * lax.rsqrt(jnp.mean(v * v, axis=-1, keepdims=True) + EPS) * gain


def silu(v):
    half = 0.5 * v
    return half + half * jnp.tanh(half)


def four(v, axis=1):
    return jnp.concatenate([v, v, v, v], axis=axis)


def packed(v, parts):
    group = lax.broadcasted_iota(jnp.int32, v.shape, 1) // 32
    rest = v
    out = jnp.zeros_like(v)
    for part in range(parts):
        piece = rest.astype(BF).astype(F32)
        out = jnp.where(group == part, piece, out)
        rest = rest - piece
    return out.astype(BF)


def expander(heads, lanes, parts):
    row = np.arange(128)[:, None]
    col = np.arange(heads * lanes)[None, :]
    return jnp.asarray((row % 32 == col // lanes) & (row < 32 * parts), BF)


def dot(a, b):
    return jnp.dot(a, b, preferred_element_type=F32)


def dot_nt(a, b):
    return lax.dot_general(a, b, (((1,), (1,)), ((), ())), preferred_element_type=F32)


def blocks(total, size):
    return [slice(i, i + size) for i in range(0, total, size)]


def call(kernel, out_shape, specs, scratch=(), flops=0, limit=12, outs=None):
    many = isinstance(out_shape, (list, tuple))
    return pl.pallas_call(
        kernel,
        in_specs=specs,
        out_specs=outs or ([VMEM] * len(out_shape) if many else VMEM),
        out_shape=out_shape,
        scratch_shapes=list(scratch),
        compiler_params=pltpu.CompilerParams(vmem_limit_bytes=limit * 1024 * 1024),
        cost_estimate=pl.CostEstimate(flops=flops, bytes_accessed=0, transcendentals=0),
    )


def shape(*dims, dtype=BF):
    return jax.ShapeDtypeStruct(dims, dtype)


def fetches(pairs, sems, started=None):
    copies = [pltpu.make_async_copy(src, dst, sems.at[i]) for i, (src, dst) in enumerate(pairs)]
    for copy in copies[:started]:
        copy.start()
    return copies


def mix_kernel(
    length, ev_h, gain_h, w_dt_h, dt_bias_h, a_log_h, halo_h, w_h, conv_w_h, conv_b_h, spread_h,
    normed_h, cum_out, cum_t, shard, chunk, x_h, bc, keep, send,
    ev, gain, w_dt, dt_bias, a_log, halo, w, conv_w, conv_b, spread,
    full, x, raw, tail, weighted, b_t, states, fades, sems, out_sems,
):
    rows, inner = x.shape
    order = [slice(inner, inner + BLK)] + blocks(inner, BLK)
    copies = fetches(
        [
            (ev_h, ev), (gain_h, gain), (w_dt_h, w_dt), (dt_bias_h, dt_bias), (a_log_h, a_log),
            (halo_h, halo), (conv_w_h, conv_w), (conv_b_h, conv_b), (spread_h, spread), (w_h, w),
        ],
        sems,
    )
    for copy in copies[:6]:
        copy.wait()
    full[:HALO] = rms(halo[...].astype(F32), gain[...]).astype(BF)
    for part in blocks(rows, PART):
        full[HALO + part.start : HALO + part.stop] = rms(ev[part].astype(F32), gain[...]).astype(BF)
    pre = dot_nt(full[HALO:], four(w_dt[...], 0))
    place = lax.axis_index(SEQ) * rows + lax.broadcasted_iota(jnp.int32, (rows, 128), 0)
    v = pre + four(dt_bias[...])
    soft = jnp.maximum(v, 0.0) + jnp.log1p(jnp.exp(-jnp.abs(v)))
    step = jnp.where(place < length[0], soft, 0.0)
    logdec = -step * jnp.exp(four(a_log[...]))
    lower = (
        lax.broadcasted_iota(jnp.int32, (rows, rows), 0)
        >= lax.broadcasted_iota(jnp.int32, (rows, rows), 1)
    ).astype(BF)
    cum = dot(lower, packed(logdec, 3))
    cum = cum + pltpu.roll(cum, 32, 1)
    cum = cum + pltpu.roll(cum, 64, 1)
    cum_out[...] = packed(cum, 3)
    flipped = jnp.transpose(cum)
    for g in range(8):
        cum_t[g] = flipped[4 * g : 4 * g + 4]
    shard[0] = packed(jnp.exp(cum[rows - 1 :] - cum) * step, 2)
    shard[1] = packed(jnp.exp(cum), 2)
    chunk[0] = packed(step, 2)
    for c, part in enumerate(blocks(rows, GROUP)):
        own = cum[part]
        chunk[1, part] = packed(jnp.exp(own[GROUP - 1 :] - own) * step[part], 2)
        chunk[2, part] = packed(jnp.exp(own - (cum[part.start - 1 : part.start] if c else 0.0)), 2)
    for copy in copies[6:]:
        copy.wait()
    stores = [pltpu.make_async_copy(full.at[HALO:], normed_h, out_sems.at[2])]
    stores[0].start()
    fades[:rows] = shard[0]
    fades[rows:] = shard[1, rows - 16 :]

    def project(n):
        both = dot(full[...], w[:, order[n]])
        raw[n % 2, 0] = both[:, :128]
        raw[n % 2, 1] = both[:, 128:]
        if n:
            tail[n % 2] = dot(fades[...], spread[:, order[n]])

    def end_state(n):
        cols = order[n]
        states[:128, cols] = dot(b_t[...], weighted[n % 2]).astype(BF)
        states[128:, cols] = jnp.broadcast_to(tail[n % 2, rows + 15 :], (16, BLK)).astype(BF)

    project(0)
    for n, cols in enumerate(order):
        slot = n % 2
        if n + 1 < len(order):
            if n > 1:
                end_state(n - 1)
            project(n + 1)
        for j in range(2):
            at = cols.start // 128 + j
            lanes = slice(at * 128, (at + 1) * 128)
            local_lanes = slice(j * 128, (j + 1) * 128)
            for part in blocks(rows, PART):
                conv = conv_b[at : at + 1]
                for k in range(4):
                    first = HALO - 3 + k + part.start
                    conv = conv + conv_w[k : k + 1, lanes] * raw[slot, j, first : first + PART]
                act = silu(conv)
                if n:
                    x[part, lanes] = act.astype(BF)
                    weighted[slot, part, local_lanes] = (act * tail[slot, part, local_lanes]).astype(BF)
                else:
                    bc[part, local_lanes] = act.astype(BF)
        if n == 0:
            b_t[...] = jnp.transpose(bc[:, :128].astype(F32)).astype(BF)
        if n == 6:
            done = slice(0, cols.stop)
            stores += fetches([(x.at[:, done], x_h.at[:, done])], out_sems.at[0:1])
    rest = slice(order[6].stop, inner)
    stores += fetches([(x.at[:, rest], x_h.at[:, rest])], out_sems.at[1:2])
    end_state(len(order) - 2)
    end_state(len(order) - 1)
    first = lax.axis_index("core") == 0
    half = inner // 2
    for part in blocks(144, 48):
        low, high = states[part, :half], states[part, half:]
        keep[part] = jnp.where(first, low, high)
        send[part] = jnp.where(first, high, low)
    for store in stores:
        store.wait()


def join(first, second, out):
    decay = second[128:129].astype(F32)
    for part in blocks(128, PART):
        out[part] = (first[part].astype(F32) * decay + second[part].astype(F32)).astype(BF)
    out[128:] = (first[128:].astype(F32) * second[128:].astype(F32)).astype(BF)


def chip_kernel(keep, got, chip):
    @pl.when(lax.axis_index("core") == 0)
    def _():
        join(keep, got, chip)

    @pl.when(lax.axis_index("core") == 1)
    def _():
        join(got, keep, chip)


def enter_kernel(keep, got, near, mid, far, here, away):
    front = lax.axis_index("core") == 0
    near_decay, mid_decay = near[128:129].astype(F32), mid[128:129].astype(F32)
    decay = jnp.where(front, keep[128:129].astype(F32), got[128:129].astype(F32))
    for part in blocks(128, PART):
        enter = mid[part].astype(F32) + mid_decay * far[part].astype(F32)
        enter = near[part].astype(F32) + near_decay * enter
        first = jnp.where(front, keep[part].astype(F32), got[part].astype(F32))
        later = first + decay * enter
        here[part] = jnp.where(front, enter, later).astype(BF)
        away[part] = jnp.where(front, later, enter).astype(BF)


def head_offsets(lanes, heads, parts):
    row = lax.broadcasted_iota(jnp.int32, (128, heads * lanes), 0)
    col = lax.broadcasted_iota(jnp.int32, (128, heads * lanes), 1)
    return jnp.where(row < 32 * parts, (row & 31) - col // lanes, -1000)


def scan_kernel(
    x, bc, cum, cum_t, chunk, d_skip, y, scores, b_t, lines, narrow, wide, steps, tails, insides, times
):
    rows, inner = x.shape
    narrow[...] = head_offsets(64, 4, 2)
    wide[...] = head_offsets(GROUP, 4, 3)
    lower = lax.broadcasted_iota(jnp.int32, (GROUP, GROUP), 0) >= lax.broadcasted_iota(
        jnp.int32, (GROUP, GROUP), 1
    )
    for c, part in enumerate(blocks(rows, GROUP)):
        scores[c] = jnp.where(lower, dot_nt(bc[part, 128:], bc[part, :128]), 0.0)
    b_t[...] = jnp.transpose(bc[:, :128].astype(F32)).astype(BF)
    lines[...] = packed(jnp.broadcast_to(four(d_skip[...]), (16, 128)), 2)
    left = lax.broadcasted_iota(jnp.int32, (GROUP, 128), 1) < 64

    def group(g, _):
        cols = pl.ds(pl.multiple_of(g * BLK, BLK), BLK)
        sp = (narrow[...] == 4 * g).astype(F32).astype(BF)
        wd = (wide[...] == 4 * g).astype(F32).astype(BF)
        skip = dot(lines[...], sp)[:1]
        before = jnp.zeros((128, BLK), F32)
        steps[...] = dot(chunk[0], sp)
        tails[...] = dot(chunk[1], sp)
        insides[...] = dot(chunk[2], sp)
        times[...] = dot(cum[...], wd)
        for c, part in enumerate(blocks(rows, GROUP)):
            xc = x[part, cols].astype(F32)
            stepped = xc * steps[part]
            inside = insides[part]
            own = times[part]
            out = xc * skip
            if c:
                out = out + dot(bc[part, 128:], before.astype(BF)) * inside
            pairs = []
            for p in range(2):
                weights = []
                for h in (2 * p, 2 * p + 1):
                    diff = own[:, h * GROUP : (h + 1) * GROUP] - cum_t[g, h : h + 1, part]
                    weights.append((scores[c] * jnp.exp(jnp.minimum(diff, 0.0))).astype(BF))
                pair = stepped[:, p * 128 : (p + 1) * 128]
                stacked = jnp.concatenate(
                    [jnp.where(left, pair, 0.0), jnp.where(left, 0.0, pair)], axis=0
                ).astype(BF)
                pairs.append(dot(jnp.concatenate(weights, axis=1), stacked))
            y[part, cols] = (out + jnp.concatenate(pairs, axis=1)).astype(BF)
            if c < rows // GROUP - 1:
                tailed = (xc * tails[part]).astype(BF)
                before = before * inside[GROUP - 1 :] + dot(b_t[:, part], tailed)
        return 0

    lax.fori_loop(0, inner // BLK, group, 0)


def out_kernel(
    y, bc, kept, got, shard, z, ev, norm_gain, w_out, final_gain, wanted, spread,
    out, picked, mixed, square, enter, total, final,
):
    rows, inner = z.shape
    width = ev.shape[1]
    half = inner // 2
    first = lax.axis_index("core") == 0
    enter[:, :half] = jnp.where(first, kept[...], got[...])
    enter[:, half:] = jnp.where(first, got[...], kept[...])
    tiles = blocks(inner, BLK)

    def spread_state(n):
        return dot(bc[:, 128:], enter[:, tiles[n]]), dot(shard[1], spread[:, tiles[n]])

    ahead = spread_state(0)
    for n, cols in enumerate(tiles):
        state, decay = ahead
        if n + 1 < len(tiles):
            ahead = spread_state(n + 1)
        for part in blocks(rows, PART):
            v = y[part, cols].astype(F32) + state[part] * decay[part]
            v = v * silu(z[part, cols].astype(F32))
            sq = v * v
            sq = sq[:, :128] + sq[:, 128:]
            square[part] = square[part] + sq if n else sq
            mixed[part, cols] = (v * norm_gain[:, cols]).astype(BF)
    for cols in blocks(width, BLK):
        total[:, cols] = dot(mixed[...], w_out[:, cols])
    for part in blocks(rows, PART):
        mean = jnp.sum(square[part], axis=1, keepdims=True) * (1.0 / inner)
        res = (ev[part].astype(F32) + total[part] * lax.rsqrt(mean + EPS)).astype(BF)
        out[part] = res
        final[part] = rms(res.astype(F32), final_gain[...]).astype(BF)
    place = lax.axis_index(SEQ) * rows + lax.broadcasted_iota(jnp.int32, (32, rows), 1)
    column = jnp.transpose(jnp.broadcast_to(wanted[...].astype(F32), (128, 32)))[:, :1]
    pick = dot((place.astype(F32) == column).astype(BF), final[...]).astype(BF)
    for s in range(8):
        picked[s] = pick[4 * s : 4 * s + 4]


def rows_kernel(ids, got, sent):
    width = got.shape[2]
    mine = got[0].astype(F32)
    for s in range(1, got.shape[0]):
        mine = mine + got[s].astype(F32)
    row = lax.broadcasted_iota(jnp.int32, (4, 128), 0)
    lane = lax.broadcasted_iota(jnp.int32, (4, 128), 1)
    own = jnp.zeros((4, 128), jnp.int32)
    for k in range(4):
        own = jnp.where(row == k, ids[0, k], own)
    digits = jnp.where(lane == 0, own >> 16, jnp.where(lane == 1, (own >> 8) & 255, own & 255))
    digits = jnp.where(lane < 3, digits, 0).astype(F32)
    both = jnp.concatenate([mine, digits], axis=1).astype(BF)
    count = sent.shape[0] // 2
    for d in range(count):
        sent[d] = both[:2]
        sent[count + d] = both[2:]


def logit_kernel(block_id, temper, own, got, items, stats, rows, ids, scale):
    count, width = own.shape[0], items.shape[1]
    tiles = blocks(items.shape[0], 512)
    first = lax.axis_index("core") == 0
    for part in blocks(count, PART):
        mine, other = own[part], got[part]
        low = jnp.where(first, mine, other)
        high = jnp.where(first, other, mine)
        rows[part] = low[:, :width]
        rows[count + part.start : count + part.stop] = high[:, :width]
    for n in range(2):
        digits = jnp.where(first == (n == 0), own[:, width:], got[:, width:]).astype(F32)
        digits = jnp.transpose(digits)
        value = digits[0:1] * 65536.0 + digits[1:2] * 256.0 + digits[2:3]
        ids[:, n * count : (n + 1) * count] = value.astype(jnp.int32)
    history = lax.broadcasted_iota(jnp.int32, scale.shape, 1) // 2 % 16
    factor = jnp.zeros(scale.shape, F32)
    for c in range(16):
        factor = jnp.where(history == c, temper[c], factor)
    scale[...] = factor
    top = jnp.full(scale.shape, -1e30, F32)
    total = jnp.zeros(scale.shape, F32)
    hit = jnp.zeros(scale.shape, F32)
    base = ids[...] - block_id[0] * items.shape[0]
    for part in tiles:
        logit = dot_nt(items[part], rows[...]) * scale[...]
        place = lax.broadcasted_iota(jnp.int32, logit.shape, 0)
        hit = hit + jnp.sum(jnp.where(place == base - part.start, logit, 0.0), axis=0, keepdims=True)
        new = jnp.maximum(top, jnp.max(logit, axis=0, keepdims=True))
        total = total * jnp.exp(top - new) + jnp.sum(jnp.exp(logit - new), axis=0, keepdims=True)
        top = new
    gap = jnp.zeros((5, count), F32)
    lines = []
    for n in range(2):
        lines += [v[:, n * count : (n + 1) * count] for v in (top, total, hit)] + [gap]
    lines = jnp.concatenate(lines + [jnp.zeros((112, count), F32)], axis=0)
    stats[...] = jnp.transpose(lines)[:, :16]


def loss_kernel(seen, loss):
    parts = []
    for n in (0, 8):
        top, total, hit = [seen[:, :, n + i : n + i + 1] for i in range(3)]
        peak = jnp.max(top, axis=0)
        whole = jnp.sum(total * jnp.exp(top - peak[None]), axis=0)
        parts.append(peak + jnp.log(whole) - jnp.sum(hit, axis=0))
    loss[...] = jnp.concatenate(parts, axis=0)


def local(
    events, lengths, target_pos, target_ids, items, item_block, temper, in_gain, w_xbc, w_z, w_dt,
    conv_w, conv_b, dt_bias, a_log, d_skip, norm_gain, w_out, final_gain,
):
    rows, width = events.shape[1:]
    inner = w_z.shape[1]
    ev = events[0]
    spread = expander(32, 64, 2)
    chunks = rows // GROUP

    with jax.named_scope("halo"):
        halo = lax.ppermute(ev[rows - HALO :], SEQ, [(i, i + 1) for i in range(7)])

    with jax.named_scope("mix"):
        normed, cum, cum_t, shard, chunk, x, bc, keep, send = call(
            mix_kernel,
            [
                shape(rows, width), shape(rows, 128), shape(8, 4, rows, dtype=F32),
                shape(2, rows, 128), shape(3, rows, 128), shape(rows, inner), shape(rows, 256),
                shape(144, inner // 2), shape(144, inner // 2),
            ],
            [SMEM] + [HBM] * 10,
            [
                pltpu.VMEM((rows, width), BF), pltpu.VMEM((1, width), F32), pltpu.VMEM((32, width), BF),
                pltpu.VMEM((1, 32), F32), pltpu.VMEM((1, 32), F32), pltpu.VMEM((HALO, width), BF),
                pltpu.VMEM(w_xbc.shape, BF), pltpu.VMEM(conv_w.shape, F32),
                pltpu.VMEM((conv_b.shape[0] // 128, 128), F32), pltpu.VMEM(spread.shape, BF),
                pltpu.VMEM((rows + HALO, width), BF), pltpu.VMEM((rows, inner), BF),
                pltpu.VMEM((2, 2, rows + HALO, 128), F32),
                pltpu.VMEM((2, rows + 16, BLK), F32), pltpu.VMEM((2, rows, BLK), BF),
                pltpu.VMEM((128, rows), BF), pltpu.VMEM((144, inner), BF), pltpu.VMEM((rows + 16, 128), BF),
                pltpu.SemaphoreType.DMA((10,)), pltpu.SemaphoreType.DMA((9,)),
            ],
            2 * rows * width * 2304,
            limit=56,
            outs=[HBM] + [VMEM] * 4 + [HBM] + [VMEM] * 3,
        )(
            lengths, ev, in_gain[None], w_dt.T, dt_bias[None], a_log[None], halo, w_xbc, conv_w,
            conv_b.reshape(-1, 128), spread,
        )

    swap = [(0, 1), (1, 0)]
    payload = shape(144, inner // 2)
    entry = shape(128, inner // 2)
    with jax.named_scope("chip"):
        got = lax.ppermute(send, "core", swap)
        chip = call(chip_kernel, payload, [VMEM] * 2)(keep, got)
        before = [
            lax.ppermute(chip, "x", [(i, i + n) for i in range(4 - n)]) for n in (1, 2, 3)
        ]
        x, chip = lax.optimization_barrier((x, chip))
    with jax.named_scope("scan"):
        y = call(
            scan_kernel,
            shape(rows, inner),
            [VMEM] * 6,
            [
                pltpu.VMEM((chunks, GROUP, GROUP), F32), pltpu.VMEM((128, rows), BF),
                pltpu.VMEM((16, 128), BF), pltpu.VMEM((128, BLK), jnp.int32),
                pltpu.VMEM((128, 4 * GROUP), jnp.int32), pltpu.VMEM((rows, BLK), F32),
                pltpu.VMEM((rows, BLK), F32), pltpu.VMEM((rows, BLK), F32), pltpu.VMEM((rows, 4 * GROUP), F32),
            ],
            16 * rows * 128 * inner,
            limit=56,
        )(x, bc, cum, cum_t, chunk, d_skip[None])
        y, source = lax.optimization_barrier((y, normed))
    with jax.named_scope("gate"):
        z = dot(source, w_z).astype(BF)
        before, z = lax.optimization_barrier((before, z))
    with jax.named_scope("enter"):
        here, away = call(enter_kernel, [entry, entry], [VMEM] * 5)(keep, got, *before)
        there = lax.ppermute(away, "core", swap)

    with jax.named_scope("out"):
        out, picked = call(
            out_kernel,
            [shape(rows, width), shape(8, 4, width)],
            [VMEM] * 12,
            [
                pltpu.VMEM((rows, inner), BF), pltpu.VMEM((rows, 128), F32), pltpu.VMEM((128, inner), BF),
                pltpu.VMEM((rows, width), F32), pltpu.VMEM((rows, width), BF),
            ],
            2 * rows * inner * (width + 256),
            limit=14,
        )(
            y, bc, here, there, shard, z, ev, norm_gain[None], w_out, final_gain[None], target_pos,
            spread,
        )

    with jax.named_scope("rows"):
        mine = lax.all_to_all(picked, SEQ, 0, 0, tiled=True)
        sent = call(rows_kernel, shape(128, 2, width + 128), [SMEM, VMEM], flops=10**10)(target_ids, mine)
        own_rows = lax.all_to_all(sent, EACH, 0, 0, tiled=True).reshape(256, width + 128)
        got_rows = lax.ppermute(own_rows, "core", swap)

    with jax.named_scope("logits"):
        stats = call(
            logit_kernel,
            shape(256, 16, dtype=F32),
            [SMEM, SMEM, VMEM, VMEM, VMEM],
            [
                pltpu.VMEM((512, width), BF), pltpu.VMEM((1, 512), jnp.int32), pltpu.VMEM((1, 512), F32),
            ],
            2 * 512 * items.shape[0] * width,
        )(item_block, temper, own_rows, got_rows, items)

    with jax.named_scope("loss"):
        seen = lax.all_to_all(stats.reshape(128, 2, 16), EACH, 0, 0, tiled=True)
        loss = call(loss_kernel, shape(4, 1, dtype=F32), [VMEM])(seen).reshape(4)
    return (out[None], loss)


def solution(mesh):
    fine = jax.sharding.Mesh(
        mesh.devices.reshape(mesh.shape["seq"] // 2, 2, mesh.shape["cand"]), ("x", "core", "cand")
    )
    each = ("x", "core", "cand")
    placed = (
        P("cand", SEQ, None),
        P("cand"),
        P("cand", None),
        P("cand", SEQ),
        P(each, None),
        P(each),
    ) + (P(),) * 13
    return jax.shard_map(
        local,
        mesh=fine,
        in_specs=placed,
        out_specs=(P("cand", SEQ, None), P(each)),
        check_vma=False,
    )
```

```python
import jax
import jax.numpy as jnp
import numpy as np
from jax import lax
from jax.experimental import pallas as pl
from jax.experimental.pallas import tpu as pltpu
from jax.sharding import PartitionSpec as P

GROUP = 128
EPS = 1e-05
BLK = 256
HALO = 16
PART = 64
LOG2E = 1.4426950408889634
BF = jnp.bfloat16
F32 = jnp.float32
SEQ = ("x", "core")
EACH = ("core", "x", "cand")
VMEM = pl.BlockSpec(memory_space=pltpu.VMEM)
HBM = pl.BlockSpec(memory_space=pl.ANY)
SMEM = pl.BlockSpec(memory_space=pltpu.SMEM)


def rms(v, gain):
    return v * lax.rsqrt(jnp.mean(v * v, axis=-1, keepdims=True) + EPS) * gain


def silu(v):
    half = 0.5 * v
    return half + half * jnp.tanh(half)


def four(v, axis=1):
    return jnp.concatenate([v, v, v, v], axis=axis)


def packed(v, parts):
    group = lax.broadcasted_iota(jnp.int32, v.shape, 1) // 32
    rest = v
    out = jnp.zeros_like(v)
    for part in range(parts):
        piece = rest.astype(BF).astype(F32)
        out = jnp.where(group == part, piece, out)
        rest = rest - piece
    return out.astype(BF)


def expander(heads, lanes, parts):
    row = np.arange(128)[:, None]
    col = np.arange(heads * lanes)[None, :]
    return jnp.asarray((row % 32 == col // lanes) & (row < 32 * parts), BF)


def dot(a, b):
    return jnp.dot(a, b, preferred_element_type=F32)


def dot_nt(a, b):
    return lax.dot_general(a, b, (((1,), (1,)), ((), ())), preferred_element_type=F32)


def blocks(total, size):
    return [slice(i, i + size) for i in range(0, total, size)]


def call(kernel, out_shape, specs, scratch=(), flops=0, limit=12, outs=None):
    many = isinstance(out_shape, (list, tuple))
    return pl.pallas_call(
        kernel,
        in_specs=specs,
        out_specs=outs or ([VMEM] * len(out_shape) if many else VMEM),
        out_shape=out_shape,
        scratch_shapes=list(scratch),
        compiler_params=pltpu.CompilerParams(vmem_limit_bytes=limit * 1024 * 1024),
        cost_estimate=pl.CostEstimate(flops=flops, bytes_accessed=0, transcendentals=0),
    )


def shape(*dims, dtype=BF):
    return jax.ShapeDtypeStruct(dims, dtype)


def fetches(pairs, sems, started=None):
    copies = [pltpu.make_async_copy(src, dst, sems.at[i]) for i, (src, dst) in enumerate(pairs)]
    for copy in copies[:started]:
        copy.start()
    return copies


def mix_kernel(
    length, ev_h, gain_h, w_dt_h, dt_bias_h, a_log_h, halo_h, w_h, conv_w_h, conv_b_h, spread_h,
    normed_h, cum_out, cum_t, shard, chunk, x_h, bc, keep, send,
    ev, gain, w_dt, dt_bias, a_log, halo, w, conv_w, conv_b, spread,
    full, x, raw, tail, weighted, b_t, states, fades, sems, out_sems,
):
    rows, inner = x.shape
    order = [slice(inner, inner + BLK)] + blocks(inner, BLK)
    copies = fetches(
        [
            (ev_h, ev), (gain_h, gain), (w_dt_h, w_dt), (dt_bias_h, dt_bias), (a_log_h, a_log),
            (halo_h, halo), (conv_w_h, conv_w), (conv_b_h, conv_b), (spread_h, spread), (w_h, w),
        ],
        sems,
    )
    for copy in copies[:6]:
        copy.wait()
    full[:HALO] = rms(halo[...].astype(F32), gain[...]).astype(BF)
    for part in blocks(rows, PART):
        full[HALO + part.start : HALO + part.stop] = rms(ev[part].astype(F32), gain[...]).astype(BF)
    pre = dot_nt(full[HALO:], four(w_dt[...], 0))
    place = lax.axis_index(SEQ) * rows + lax.broadcasted_iota(jnp.int32, (rows, 128), 0)
    v = pre + four(dt_bias[...])
    soft = jnp.maximum(v, 0.0) + jnp.log1p(jnp.exp(-jnp.abs(v)))
    step = jnp.where(place < length[0], soft, 0.0)
    logdec = -step * jnp.exp(four(a_log[...]))
    lower = (
        lax.broadcasted_iota(jnp.int32, (rows, rows), 0)
        >= lax.broadcasted_iota(jnp.int32, (rows, rows), 1)
    ).astype(BF)
    cum = dot(lower, packed(logdec, 3))
    cum = cum + pltpu.roll(cum, 32, 1)
    cum = cum + pltpu.roll(cum, 64, 1)
    scaled = cum * LOG2E
    cum_out[...] = packed(scaled, 3)
    flipped = jnp.transpose(scaled)
    for g in range(8):
        cum_t[g] = flipped[4 * g : 4 * g + 4]
    shard[0] = packed(jnp.exp(cum[rows - 1 :] - cum) * step, 2)
    shard[1] = packed(jnp.exp(cum), 2)
    chunk[0] = packed(step, 2)
    for c, part in enumerate(blocks(rows, GROUP)):
        own = cum[part]
        chunk[1, part] = packed(jnp.exp(own[GROUP - 1 :] - own) * step[part], 2)
        chunk[2, part] = packed(jnp.exp(own - (cum[part.start - 1 : part.start] if c else 0.0)), 2)
    for copy in copies[6:]:
        copy.wait()
    stores = [pltpu.make_async_copy(full.at[HALO:], normed_h, out_sems.at[2])]
    stores[0].start()
    fades[:rows] = shard[0]
    fades[rows:] = shard[1, rows - 16 :]

    def project(n):
        both = dot(full[...], w[:, order[n]])
        raw[n % 2, 0] = both[:, :128]
        raw[n % 2, 1] = both[:, 128:]
        if n:
            tail[n % 2] = dot(fades[...], spread[:, order[n]])

    def end_state(n):
        cols = order[n]
        states[:128, cols] = dot(b_t[...], weighted[n % 2]).astype(BF)
        states[128:, cols] = jnp.broadcast_to(tail[n % 2, rows + 15 :], (16, BLK)).astype(BF)

    project(0)
    for n, cols in enumerate(order):
        slot = n % 2
        if n + 1 < len(order):
            if n > 1:
                end_state(n - 1)
            project(n + 1)
        for j in range(2):
            at = cols.start // 128 + j
            lanes = slice(at * 128, (at + 1) * 128)
            local_lanes = slice(j * 128, (j + 1) * 128)
            for part in blocks(rows, PART):
                conv = conv_b[at : at + 1]
                for k in range(4):
                    first = HALO - 3 + k + part.start
                    conv = conv + conv_w[k : k + 1, lanes] * raw[slot, j, first : first + PART]
                act = silu(conv)
                if n:
                    x[part, lanes] = act.astype(BF)
                    weighted[slot, part, local_lanes] = (act * tail[slot, part, local_lanes]).astype(BF)
                else:
                    bc[part, local_lanes] = act.astype(BF)
        if n == 0:
            b_t[...] = jnp.transpose(bc[:, :128].astype(F32)).astype(BF)
        if n == 6:
            done = slice(0, cols.stop)
            stores += fetches([(x.at[:, done], x_h.at[:, done])], out_sems.at[0:1])
    rest = slice(order[6].stop, inner)
    stores += fetches([(x.at[:, rest], x_h.at[:, rest])], out_sems.at[1:2])
    end_state(len(order) - 2)
    end_state(len(order) - 1)
    first = lax.axis_index("core") == 0
    half = inner // 2
    for part in blocks(144, 48):
        low, high = states[part, :half], states[part, half:]
        keep[part] = jnp.where(first, low, high)
        send[part] = jnp.where(first, high, low)
    for store in stores:
        store.wait()


def join(first, second, out):
    decay = second[128:129].astype(F32)
    for part in blocks(128, PART):
        out[part] = (first[part].astype(F32) * decay + second[part].astype(F32)).astype(BF)
    out[128:] = (first[128:].astype(F32) * second[128:].astype(F32)).astype(BF)


def chip_kernel(keep, got, chip):
    @pl.when(lax.axis_index("core") == 0)
    def _():
        join(keep, got, chip)

    @pl.when(lax.axis_index("core") == 1)
    def _():
        join(got, keep, chip)


def enter_kernel(keep, got, near, mid, far, here, away):
    front = lax.axis_index("core") == 0
    near_decay, mid_decay = near[128:129].astype(F32), mid[128:129].astype(F32)
    decay = jnp.where(front, keep[128:129].astype(F32), got[128:129].astype(F32))
    for part in blocks(128, PART):
        enter = mid[part].astype(F32) + mid_decay * far[part].astype(F32)
        enter = near[part].astype(F32) + near_decay * enter
        first = jnp.where(front, keep[part].astype(F32), got[part].astype(F32))
        later = first + decay * enter
        here[part] = jnp.where(front, enter, later).astype(BF)
        away[part] = jnp.where(front, later, enter).astype(BF)


def head_offsets(lanes, heads, parts):
    row = lax.broadcasted_iota(jnp.int32, (128, heads * lanes), 0)
    col = lax.broadcasted_iota(jnp.int32, (128, heads * lanes), 1)
    return jnp.where(row < 32 * parts, (row & 31) - col // lanes, -1000)


def scan_kernel(
    x, bc, cum, cum_t, chunk, d_skip, y, scores, b_t, firsts, narrow, wide, steps, tails, insides, times
):
    rows, inner = x.shape
    narrow[...] = head_offsets(64, 4, 2)
    wide[...] = head_offsets(GROUP, 4, 3)
    lower = lax.broadcasted_iota(jnp.int32, (GROUP, GROUP), 0) >= lax.broadcasted_iota(
        jnp.int32, (GROUP, GROUP), 1
    )
    parts = blocks(rows, GROUP)
    for c, part in enumerate(parts):
        scores[c] = jnp.where(lower, dot_nt(bc[part, 128:], bc[part, :128]), 0.0).astype(BF)
    b_t[...] = jnp.transpose(bc[:, :128].astype(F32)).astype(BF)
    firsts[:rows] = chunk[0]
    firsts[rows:] = packed(jnp.broadcast_to(four(d_skip[...]), (16, 128)), 2)
    left = (lax.broadcasted_iota(jnp.int32, (GROUP, 128), 1) < 64).astype(F32).astype(BF)
    right = (lax.broadcasted_iota(jnp.int32, (GROUP, 128), 1) >= 64).astype(F32).astype(BF)

    def widen(g):
        slot = g % 2
        sp = (narrow[...] == 4 * g).astype(F32).astype(BF)
        wd = (wide[...] == 4 * g).astype(F32).astype(BF)
        steps[slot] = dot(firsts[...], sp)
        tails[slot] = dot(chunk[1], sp)
        insides[slot] = dot(chunk[2], sp)
        times[slot] = dot(cum[...], wd)

    def group(g):
        slot = g % 2
        cols = slice(g * BLK, (g + 1) * BLK)
        skip = steps[slot, rows : rows + 1]
        before = None
        entering = [None]
        for part in parts[:-1]:
            tailed = (x[part, cols].astype(F32) * tails[slot, part]).astype(BF)
            new = dot(b_t[:, part], tailed)
            before = new if before is None else before * insides[slot, part.stop - 1 : part.stop] + new
            entering.append(before.astype(BF))
        for c, part in enumerate(parts):
            xc = x[part, cols].astype(F32)
            stepped = (xc * steps[slot, part]).astype(BF)
            out = xc * skip
            if c:
                out = out + dot(bc[part, 128:], entering[c]) * insides[slot, part]
            pairs = []
            for p in range(2):
                weights = []
                for h in (2 * p, 2 * p + 1):
                    diff = times[slot, part, h * GROUP : (h + 1) * GROUP] - cum_t[g, h : h + 1, part]
                    weights.append(jnp.exp2(jnp.minimum(diff, 0.0)).astype(BF) * scores[c])
                pair = stepped[:, p * 128 : (p + 1) * 128]
                stacked = jnp.concatenate([pair * left, pair * right], axis=0)
                pairs.append(dot(jnp.concatenate(weights, axis=1), stacked))
            y[part, cols] = (out + jnp.concatenate(pairs, axis=1)).astype(BF)

    widen(0)
    for g in range(inner // BLK):
        if g + 1 < inner // BLK:
            widen(g + 1)
        group(g)


def out_kernel(
    y, bc, kept, got, shard, z, ev, norm_gain, w_out, final_gain, wanted, spread,
    out, picked, mixed, square, enter, total, final,
):
    rows, inner = z.shape
    width = ev.shape[1]
    half = inner // 2
    first = lax.axis_index("core") == 0
    enter[:, :half] = jnp.where(first, kept[...], got[...])
    enter[:, half:] = jnp.where(first, got[...], kept[...])
    tiles = blocks(inner, BLK)

    def spread_state(n):
        return dot(bc[:, 128:], enter[:, tiles[n]]), dot(shard[1], spread[:, tiles[n]])

    ahead = spread_state(0)
    for n, cols in enumerate(tiles):
        state, decay = ahead
        if n + 1 < len(tiles):
            ahead = spread_state(n + 1)
        for part in blocks(rows, PART):
            v = y[part, cols].astype(F32) + state[part] * decay[part]
            v = v * silu(z[part, cols].astype(F32))
            sq = v * v
            sq = sq[:, :128] + sq[:, 128:]
            square[part] = square[part] + sq if n else sq
            mixed[part, cols] = (v * norm_gain[:, cols]).astype(BF)
    for cols in blocks(width, BLK):
        total[:, cols] = dot(mixed[...], w_out[:, cols])
    for part in blocks(rows, PART):
        mean = jnp.sum(square[part], axis=1, keepdims=True) * (1.0 / inner)
        res = (ev[part].astype(F32) + total[part] * lax.rsqrt(mean + EPS)).astype(BF)
        out[part] = res
        final[part] = rms(res.astype(F32), final_gain[...]).astype(BF)
    place = lax.axis_index(SEQ) * rows + lax.broadcasted_iota(jnp.int32, (32, rows), 1)
    column = jnp.transpose(jnp.broadcast_to(wanted[...].astype(F32), (128, 32)))[:, :1]
    pick = dot((place.astype(F32) == column).astype(BF), final[...]).astype(BF)
    for s in range(8):
        picked[s] = pick[4 * s : 4 * s + 4]


def rows_kernel(ids, got, sent):
    width = got.shape[2]
    mine = got[0].astype(F32)
    for s in range(1, got.shape[0]):
        mine = mine + got[s].astype(F32)
    row = lax.broadcasted_iota(jnp.int32, (4, 128), 0)
    lane = lax.broadcasted_iota(jnp.int32, (4, 128), 1)
    own = jnp.zeros((4, 128), jnp.int32)
    for k in range(4):
        own = jnp.where(row == k, ids[0, k], own)
    digits = jnp.where(lane == 0, own >> 16, jnp.where(lane == 1, (own >> 8) & 255, own & 255))
    digits = jnp.where(lane < 3, digits, 0).astype(F32)
    both = jnp.concatenate([mine, digits], axis=1).astype(BF)
    count = sent.shape[0] // 2
    for d in range(count):
        sent[d] = both[:2]
        sent[count + d] = both[2:]


def logit_kernel(block_id, temper, own, got, items, stats, rows, ids, scale):
    count, width = own.shape[0], items.shape[1]
    tiles = blocks(items.shape[0], 512)
    first = lax.axis_index("core") == 0
    for part in blocks(count, PART):
        mine, other = own[part], got[part]
        low = jnp.where(first, mine, other)
        high = jnp.where(first, other, mine)
        rows[part] = low[:, :width]
        rows[count + part.start : count + part.stop] = high[:, :width]
    for n in range(2):
        digits = jnp.where(first == (n == 0), own[:, width:], got[:, width:]).astype(F32)
        digits = jnp.transpose(digits)
        value = digits[0:1] * 65536.0 + digits[1:2] * 256.0 + digits[2:3]
        ids[:, n * count : (n + 1) * count] = value.astype(jnp.int32)
    history = lax.broadcasted_iota(jnp.int32, scale.shape, 1) // 2 % 16
    factor = jnp.zeros(scale.shape, F32)
    for c in range(16):
        factor = jnp.where(history == c, temper[c], factor)
    scale[...] = factor
    top = jnp.full(scale.shape, -1e30, F32)
    total = jnp.zeros(scale.shape, F32)
    hit = jnp.zeros(scale.shape, F32)
    base = ids[...] - block_id[0] * items.shape[0]
    for part in tiles:
        logit = dot_nt(items[part], rows[...]) * scale[...]
        place = lax.broadcasted_iota(jnp.int32, logit.shape, 0)
        hit = hit + jnp.sum(jnp.where(place == base - part.start, logit, 0.0), axis=0, keepdims=True)
        new = jnp.maximum(top, jnp.max(logit, axis=0, keepdims=True))
        total = total * jnp.exp(top - new) + jnp.sum(jnp.exp(logit - new), axis=0, keepdims=True)
        top = new
    gap = jnp.zeros((5, count), F32)
    lines = []
    for n in range(2):
        lines += [v[:, n * count : (n + 1) * count] for v in (top, total, hit)] + [gap]
    lines = jnp.concatenate(lines + [jnp.zeros((112, count), F32)], axis=0)
    stats[...] = jnp.transpose(lines)[:, :16]


def loss_kernel(seen, loss):
    parts = []
    for n in (0, 8):
        top, total, hit = [seen[:, :, n + i : n + i + 1] for i in range(3)]
        peak = jnp.max(top, axis=0)
        whole = jnp.sum(total * jnp.exp(top - peak[None]), axis=0)
        parts.append(peak + jnp.log(whole) - jnp.sum(hit, axis=0))
    loss[...] = jnp.concatenate([p[k : k + 1] for p in parts for k in range(2)], axis=1)


def local(
    events, lengths, target_pos, target_ids, items, item_block, temper, in_gain, w_xbc, w_z, w_dt,
    conv_w, conv_b, dt_bias, a_log, d_skip, norm_gain, w_out, final_gain,
):
    rows, width = events.shape[1:]
    inner = w_z.shape[1]
    ev = events[0]
    spread = expander(32, 64, 2)
    chunks = rows // GROUP

    with jax.named_scope("halo"):
        halo = lax.ppermute(ev[rows - HALO :], SEQ, [(i, i + 1) for i in range(7)])

    with jax.named_scope("mix"):
        normed, cum, cum_t, shard, chunk, x, bc, keep, send = call(
            mix_kernel,
            [
                shape(rows, width), shape(rows, 128), shape(8, 4, rows, dtype=F32),
                shape(2, rows, 128), shape(3, rows, 128), shape(rows, inner), shape(rows, 256),
                shape(144, inner // 2), shape(144, inner // 2),
            ],
            [SMEM] + [HBM] * 10,
            [
                pltpu.VMEM((rows, width), BF), pltpu.VMEM((1, width), F32), pltpu.VMEM((32, width), BF),
                pltpu.VMEM((1, 32), F32), pltpu.VMEM((1, 32), F32), pltpu.VMEM((HALO, width), BF),
                pltpu.VMEM(w_xbc.shape, BF), pltpu.VMEM(conv_w.shape, F32),
                pltpu.VMEM((conv_b.shape[0] // 128, 128), F32), pltpu.VMEM(spread.shape, BF),
                pltpu.VMEM((rows + HALO, width), BF), pltpu.VMEM((rows, inner), BF),
                pltpu.VMEM((2, 2, rows + HALO, 128), F32),
                pltpu.VMEM((2, rows + 16, BLK), F32), pltpu.VMEM((2, rows, BLK), BF),
                pltpu.VMEM((128, rows), BF), pltpu.VMEM((144, inner), BF), pltpu.VMEM((rows + 16, 128), BF),
                pltpu.SemaphoreType.DMA((10,)), pltpu.SemaphoreType.DMA((9,)),
            ],
            2 * rows * width * 2304,
            limit=56,
            outs=[HBM] + [VMEM] * 4 + [HBM] + [VMEM] * 3,
        )(
            lengths, ev, in_gain[None], w_dt.T, dt_bias[None], a_log[None], halo, w_xbc, conv_w,
            conv_b.reshape(-1, 128), spread,
        )

    swap = [(0, 1), (1, 0)]
    payload = shape(144, inner // 2)
    entry = shape(128, inner // 2)
    with jax.named_scope("chip"):
        got = lax.ppermute(send, "core", swap)
        chip = call(chip_kernel, payload, [VMEM] * 2)(keep, got)
        before = [
            lax.ppermute(chip, "x", [(i, i + n) for i in range(4 - n)]) for n in (1, 2, 3)
        ]
        x, chip = lax.optimization_barrier((x, chip))
    with jax.named_scope("scan"):
        y = call(
            scan_kernel,
            shape(rows, inner),
            [VMEM] * 6,
            [
                pltpu.VMEM((chunks, GROUP, GROUP), BF), pltpu.VMEM((128, rows), BF),
                pltpu.VMEM((rows + 16, 128), BF), pltpu.VMEM((128, BLK), jnp.int32),
                pltpu.VMEM((128, 4 * GROUP), jnp.int32), pltpu.VMEM((2, rows + 16, BLK), F32),
                pltpu.VMEM((2, rows, BLK), F32), pltpu.VMEM((2, rows, BLK), F32),
                pltpu.VMEM((2, rows, 4 * GROUP), F32),
            ],
            16 * rows * 128 * inner,
            limit=56,
        )(x, bc, cum, cum_t, chunk, d_skip[None])
        y, source = lax.optimization_barrier((y, normed))
    with jax.named_scope("gate"):
        z = dot(source, w_z).astype(BF)
        before, z = lax.optimization_barrier((before, z))
    with jax.named_scope("enter"):
        here, away = call(enter_kernel, [entry, entry], [VMEM] * 5)(keep, got, *before)
        there = lax.ppermute(away, "core", swap)

    with jax.named_scope("out"):
        out, picked = call(
            out_kernel,
            [shape(rows, width), shape(8, 4, width)],
            [VMEM] * 12,
            [
                pltpu.VMEM((rows, inner), BF), pltpu.VMEM((rows, 128), F32), pltpu.VMEM((128, inner), BF),
                pltpu.VMEM((rows, width), F32), pltpu.VMEM((rows, width), BF),
            ],
            2 * rows * inner * (width + 256),
            limit=14,
        )(
            y, bc, here, there, shard, z, ev, norm_gain[None], w_out, final_gain[None], target_pos,
            spread,
        )

    with jax.named_scope("rows"):
        mine = lax.all_to_all(picked, SEQ, 0, 0, tiled=True)
        sent = call(rows_kernel, shape(128, 2, width + 128), [SMEM, VMEM])(target_ids, mine)
        own_rows = lax.all_to_all(sent, EACH, 0, 0, tiled=True).reshape(256, width + 128)
        got_rows = lax.ppermute(own_rows, "core", swap)

    with jax.named_scope("logits"):
        stats = call(
            logit_kernel,
            shape(256, 16, dtype=F32),
            [SMEM, SMEM, VMEM, VMEM, VMEM],
            [
                pltpu.VMEM((512, width), BF), pltpu.VMEM((1, 512), jnp.int32), pltpu.VMEM((1, 512), F32),
            ],
            2 * 512 * items.shape[0] * width,
        )(item_block, temper, own_rows, got_rows, items)

    with jax.named_scope("loss"):
        seen = lax.all_to_all(stats.reshape(128, 2, 16), EACH, 0, 0, tiled=True)
        loss = call(loss_kernel, shape(1, 4, dtype=F32), [VMEM])(seen).reshape(4)
    return (out[None], loss)


def solution(mesh):
    fine = jax.sharding.Mesh(
        mesh.devices.reshape(mesh.shape["seq"] // 2, 2, mesh.shape["cand"]), ("x", "core", "cand")
    )
    each = ("x", "core", "cand")
    placed = (
        P("cand", SEQ, None),
        P("cand"),
        P("cand", None),
        P("cand", SEQ),
        P(each, None),
        P(each),
    ) + (P(),) * 13
    return jax.shard_map(
        local,
        mesh=fine,
        in_specs=placed,
        out_specs=(P("cand", SEQ, None), P(each)),
        check_vma=False,
    )
```

```python
import jax
import jax.numpy as jnp
import numpy as np
from jax import lax
from jax.experimental import pallas as pl
from jax.experimental.pallas import tpu as pltpu
from jax.sharding import PartitionSpec as P

GROUP = 128
EPS = 1e-05
BLK = 256
HALO = 16
PART = 64
LOG2E = 1.4426950408889634
BF = jnp.bfloat16
F32 = jnp.float32
SEQ = ("x", "core")
EACH = ("core", "x", "cand")
VMEM = pl.BlockSpec(memory_space=pltpu.VMEM)
HBM = pl.BlockSpec(memory_space=pl.ANY)
SMEM = pl.BlockSpec(memory_space=pltpu.SMEM)


def rms(v, gain):
    return v * lax.rsqrt(jnp.mean(v * v, axis=-1, keepdims=True) + EPS) * gain


def silu(v):
    half = 0.5 * v
    return half + half * jnp.tanh(half)


def four(v, axis=1):
    return jnp.concatenate([v, v, v, v], axis=axis)


def packed(v, parts):
    group = lax.broadcasted_iota(jnp.int32, v.shape, 1) // 32
    rest = v
    out = jnp.zeros_like(v)
    for part in range(parts):
        piece = rest.astype(BF).astype(F32)
        out = jnp.where(group == part, piece, out)
        rest = rest - piece
    return out.astype(BF)


def expander(heads, lanes, parts):
    row = np.arange(128)[:, None]
    col = np.arange(heads * lanes)[None, :]
    return jnp.asarray((row % 32 == col // lanes) & (row < 32 * parts), BF)


def dot(a, b):
    return jnp.dot(a, b, preferred_element_type=F32)


def dot_nt(a, b):
    return lax.dot_general(a, b, (((1,), (1,)), ((), ())), preferred_element_type=F32)


def blocks(total, size):
    return [slice(i, i + size) for i in range(0, total, size)]


def call(kernel, out_shape, specs, scratch=(), flops=0, limit=12, outs=None):
    many = isinstance(out_shape, (list, tuple))
    return pl.pallas_call(
        kernel,
        in_specs=specs,
        out_specs=outs or ([VMEM] * len(out_shape) if many else VMEM),
        out_shape=out_shape,
        scratch_shapes=list(scratch),
        compiler_params=pltpu.CompilerParams(vmem_limit_bytes=limit * 1024 * 1024),
        cost_estimate=pl.CostEstimate(flops=flops, bytes_accessed=0, transcendentals=0),
    )


def shape(*dims, dtype=BF):
    return jax.ShapeDtypeStruct(dims, dtype)


def fetches(pairs, sems, started=None):
    copies = [pltpu.make_async_copy(src, dst, sems.at[i]) for i, (src, dst) in enumerate(pairs)]
    for copy in copies[:started]:
        copy.start()
    return copies


def mix_kernel(
    length, ev_h, gain_h, w_dt_h, dt_bias_h, a_log_h, halo_h, w_h, conv_w_h, conv_b_h, spread_h,
    normed_h, cum_out, cum_t, shard, chunk, x_h, bc, keep, send,
    ev, gain, w_dt, dt_bias, a_log, halo, w, conv_w, conv_b, spread,
    full, x, raw, tail, weighted, b_t, states, fades, sems, out_sems,
):
    rows, inner = x.shape
    order = [slice(inner, inner + BLK)] + blocks(inner, BLK)
    copies = fetches(
        [
            (ev_h, ev), (gain_h, gain), (w_dt_h, w_dt), (dt_bias_h, dt_bias), (a_log_h, a_log),
            (halo_h, halo), (conv_w_h, conv_w), (conv_b_h, conv_b), (spread_h, spread), (w_h, w),
        ],
        sems,
    )
    for copy in copies[:6]:
        copy.wait()
    full[:HALO] = rms(halo[...].astype(F32), gain[...]).astype(BF)
    for part in blocks(rows, PART):
        full[HALO + part.start : HALO + part.stop] = rms(ev[part].astype(F32), gain[...]).astype(BF)
    pre = dot_nt(full[HALO:], four(w_dt[...], 0))
    place = lax.axis_index(SEQ) * rows + lax.broadcasted_iota(jnp.int32, (rows, 128), 0)
    v = pre + four(dt_bias[...])
    soft = jnp.maximum(v, 0.0) + jnp.log1p(jnp.exp(-jnp.abs(v)))
    step = jnp.where(place < length[0], soft, 0.0)
    logdec = -step * jnp.exp(four(a_log[...]))
    lower = (
        lax.broadcasted_iota(jnp.int32, (rows, rows), 0)
        >= lax.broadcasted_iota(jnp.int32, (rows, rows), 1)
    ).astype(BF)
    cum = dot(lower, packed(logdec, 3))
    cum = cum + pltpu.roll(cum, 32, 1)
    cum = cum + pltpu.roll(cum, 64, 1)
    scaled = cum * LOG2E
    cum_out[...] = packed(scaled, 3)
    flipped = jnp.transpose(scaled)
    for g in range(8):
        cum_t[g] = flipped[4 * g : 4 * g + 4]
    shard[0] = packed(jnp.exp(cum[rows - 1 :] - cum) * step, 2)
    shard[1] = packed(jnp.exp(cum), 2)
    chunk[0] = packed(step, 2)
    for c, part in enumerate(blocks(rows, GROUP)):
        own = cum[part]
        chunk[1, part] = packed(jnp.exp(own[GROUP - 1 :] - own) * step[part], 2)
        chunk[2, part] = packed(jnp.exp(own - (cum[part.start - 1 : part.start] if c else 0.0)), 2)
    for copy in copies[6:]:
        copy.wait()
    stores = [pltpu.make_async_copy(full.at[HALO:], normed_h, out_sems.at[2])]
    stores[0].start()
    fades[:rows] = shard[0]
    fades[rows:] = shard[1, rows - 16 :]

    def project(n):
        both = dot(full[...], w[:, order[n]])
        raw[n % 2, 0] = both[:, :128]
        raw[n % 2, 1] = both[:, 128:]
        if n:
            tail[n % 2] = dot(fades[...], spread[:, order[n]])

    def end_state(n):
        cols = order[n]
        states[:128, cols] = dot(b_t[...], weighted[n % 2]).astype(BF)
        states[128:, cols] = jnp.broadcast_to(tail[n % 2, rows + 15 :], (16, BLK)).astype(BF)

    project(0)
    for n, cols in enumerate(order):
        slot = n % 2
        if n + 1 < len(order):
            if n > 1:
                end_state(n - 1)
            project(n + 1)
        for j in range(2):
            at = cols.start // 128 + j
            lanes = slice(at * 128, (at + 1) * 128)
            local_lanes = slice(j * 128, (j + 1) * 128)
            for part in blocks(rows, PART):
                conv = conv_b[at : at + 1]
                for k in range(4):
                    first = HALO - 3 + k + part.start
                    conv = conv + conv_w[k : k + 1, lanes] * raw[slot, j, first : first + PART]
                act = silu(conv)
                if n:
                    x[part, lanes] = act.astype(BF)
                    weighted[slot, part, local_lanes] = (act * tail[slot, part, local_lanes]).astype(BF)
                else:
                    bc[part, local_lanes] = act.astype(BF)
        if n == 0:
            b_t[...] = jnp.transpose(bc[:, :128].astype(F32)).astype(BF)
        if n == 6:
            done = slice(0, cols.stop)
            stores += fetches([(x.at[:, done], x_h.at[:, done])], out_sems.at[0:1])
    rest = slice(order[6].stop, inner)
    stores += fetches([(x.at[:, rest], x_h.at[:, rest])], out_sems.at[1:2])
    end_state(len(order) - 2)
    end_state(len(order) - 1)
    first = lax.axis_index("core") == 0
    half = inner // 2
    for part in blocks(144, 48):
        low, high = states[part, :half], states[part, half:]
        keep[part] = jnp.where(first, low, high)
        send[part] = jnp.where(first, high, low)
    for store in stores:
        store.wait()


def join(first, second, out):
    decay = second[128:129].astype(F32)
    for part in blocks(128, PART):
        out[part] = (first[part].astype(F32) * decay + second[part].astype(F32)).astype(BF)
    out[128:] = (first[128:].astype(F32) * second[128:].astype(F32)).astype(BF)


def hold_kernel(keep, held):
    for part in blocks(keep.shape[0], 16):
        held[part] = keep[part]


def chip_kernel(keep, got, chip):
    @pl.when(lax.axis_index("core") == 0)
    def _():
        join(keep, got, chip)

    @pl.when(lax.axis_index("core") == 1)
    def _():
        join(got, keep, chip)


def enter_kernel(keep, got, near, mid, far, here, away):
    front = lax.axis_index("core") == 0
    near_decay, mid_decay = near[128:129].astype(F32), mid[128:129].astype(F32)
    decay = jnp.where(front, keep[128:129].astype(F32), got[128:129].astype(F32))
    for part in blocks(128, PART):
        enter = mid[part].astype(F32) + mid_decay * far[part].astype(F32)
        enter = near[part].astype(F32) + near_decay * enter
        first = jnp.where(front, keep[part].astype(F32), got[part].astype(F32))
        later = first + decay * enter
        here[part] = jnp.where(front, enter, later).astype(BF)
        away[part] = jnp.where(front, later, enter).astype(BF)


def head_offsets(lanes, heads, parts):
    row = lax.broadcasted_iota(jnp.int32, (128, heads * lanes), 0)
    col = lax.broadcasted_iota(jnp.int32, (128, heads * lanes), 1)
    return jnp.where(row < 32 * parts, (row & 31) - col // lanes, -1000)


def scan_kernel(
    x, bc, cum, cum_t, chunk, d_skip, y, scores, b_t, firsts, narrow, wide, steps, tails, insides, times
):
    rows, inner = x.shape
    narrow[...] = head_offsets(64, 4, 2)
    wide[...] = head_offsets(GROUP, 4, 3)
    lower = lax.broadcasted_iota(jnp.int32, (GROUP, GROUP), 0) >= lax.broadcasted_iota(
        jnp.int32, (GROUP, GROUP), 1
    )
    parts = blocks(rows, GROUP)
    for c, part in enumerate(parts):
        scores[c] = jnp.where(lower, dot_nt(bc[part, 128:], bc[part, :128]), 0.0).astype(BF)
    b_t[...] = jnp.transpose(bc[:, :128].astype(F32)).astype(BF)
    firsts[:rows] = chunk[0]
    firsts[rows:] = packed(jnp.broadcast_to(four(d_skip[...]), (16, 128)), 2)
    left = (lax.broadcasted_iota(jnp.int32, (GROUP, 128), 1) < 64).astype(F32).astype(BF)
    right = (lax.broadcasted_iota(jnp.int32, (GROUP, 128), 1) >= 64).astype(F32).astype(BF)

    def widen(g):
        slot = g % 2
        sp = (narrow[...] == 4 * g).astype(F32).astype(BF)
        wd = (wide[...] == 4 * g).astype(F32).astype(BF)
        steps[slot] = dot(firsts[...], sp)
        tails[slot] = dot(chunk[1], sp)
        insides[slot] = dot(chunk[2], sp)
        times[slot] = dot(cum[...], wd)

    def group(g):
        slot = g % 2
        cols = slice(g * BLK, (g + 1) * BLK)
        skip = steps[slot, rows : rows + 1]
        before = None
        entering = [None]
        for part in parts[:-1]:
            tailed = (x[part, cols].astype(F32) * tails[slot, part]).astype(BF)
            new = dot(b_t[:, part], tailed)
            before = new if before is None else before * insides[slot, part.stop - 1 : part.stop] + new
            entering.append(before.astype(BF))
        for c, part in enumerate(parts):
            xc = x[part, cols].astype(F32)
            stepped = (xc * steps[slot, part]).astype(BF)
            out = xc * skip
            if c:
                out = out + dot(bc[part, 128:], entering[c]) * insides[slot, part]
            pairs = []
            for p in range(2):
                weights = []
                for h in (2 * p, 2 * p + 1):
                    diff = times[slot, part, h * GROUP : (h + 1) * GROUP] - cum_t[g, h : h + 1, part]
                    weights.append(jnp.exp2(jnp.minimum(diff, 0.0)).astype(BF) * scores[c])
                pair = stepped[:, p * 128 : (p + 1) * 128]
                stacked = jnp.concatenate([pair * left, pair * right], axis=0)
                pairs.append(dot(jnp.concatenate(weights, axis=1), stacked))
            y[part, cols] = (out + jnp.concatenate(pairs, axis=1)).astype(BF)

    widen(0)
    for g in range(inner // BLK):
        if g + 1 < inner // BLK:
            widen(g + 1)
        group(g)


def out_kernel(
    y, bc, kept, got, shard, z, ev, norm_gain, w_out, final_gain, wanted, spread,
    out, picked, mixed, square, enter, total, final,
):
    rows, inner = z.shape
    width = ev.shape[1]
    half = inner // 2
    first = lax.axis_index("core") == 0
    enter[:, :half] = jnp.where(first, kept[...], got[...])
    enter[:, half:] = jnp.where(first, got[...], kept[...])
    tiles = blocks(inner, BLK)

    def spread_state(n):
        return dot(bc[:, 128:], enter[:, tiles[n]]), dot(shard[1], spread[:, tiles[n]])

    ahead = spread_state(0)
    for n, cols in enumerate(tiles):
        state, decay = ahead
        if n + 1 < len(tiles):
            ahead = spread_state(n + 1)
        for part in blocks(rows, PART):
            v = y[part, cols].astype(F32) + state[part] * decay[part]
            v = v * silu(z[part, cols].astype(F32))
            sq = v * v
            sq = sq[:, :128] + sq[:, 128:]
            square[part] = square[part] + sq if n else sq
            mixed[part, cols] = (v * norm_gain[:, cols]).astype(BF)
    for cols in blocks(width, BLK):
        total[:, cols] = dot(mixed[...], w_out[:, cols])
    for part in blocks(rows, PART):
        mean = jnp.sum(square[part], axis=1, keepdims=True) * (1.0 / inner)
        res = (ev[part].astype(F32) + total[part] * lax.rsqrt(mean + EPS)).astype(BF)
        out[part] = res
        final[part] = rms(res.astype(F32), final_gain[...]).astype(BF)
    place = lax.axis_index(SEQ) * rows + lax.broadcasted_iota(jnp.int32, (32, rows), 1)
    column = jnp.transpose(jnp.broadcast_to(wanted[...].astype(F32), (128, 32)))[:, :1]
    pick = dot((place.astype(F32) == column).astype(BF), final[...]).astype(BF)
    for s in range(8):
        picked[s] = pick[4 * s : 4 * s + 4]


def rows_kernel(ids, got, sent):
    width = got.shape[2]
    mine = got[0].astype(F32)
    for s in range(1, got.shape[0]):
        mine = mine + got[s].astype(F32)
    row = lax.broadcasted_iota(jnp.int32, (4, 128), 0)
    lane = lax.broadcasted_iota(jnp.int32, (4, 128), 1)
    own = jnp.zeros((4, 128), jnp.int32)
    for k in range(4):
        own = jnp.where(row == k, ids[0, k], own)
    digits = jnp.where(lane == 0, own >> 16, jnp.where(lane == 1, (own >> 8) & 255, own & 255))
    digits = jnp.where(lane < 3, digits, 0).astype(F32)
    both = jnp.concatenate([mine, digits], axis=1).astype(BF)
    count = sent.shape[0] // 2
    for d in range(count):
        sent[d] = both[:2]
        sent[count + d] = both[2:]


def logit_kernel(block_id, temper, own, got, items, stats, rows, ids, scale):
    count, width = own.shape[0], items.shape[1]
    tiles = blocks(items.shape[0], 512)
    first = lax.axis_index("core") == 0
    for part in blocks(count, PART):
        mine, other = own[part], got[part]
        low = jnp.where(first, mine, other)
        high = jnp.where(first, other, mine)
        rows[part] = low[:, :width]
        rows[count + part.start : count + part.stop] = high[:, :width]
    for n in range(2):
        digits = jnp.where(first == (n == 0), own[:, width:], got[:, width:]).astype(F32)
        digits = jnp.transpose(digits)
        value = digits[0:1] * 65536.0 + digits[1:2] * 256.0 + digits[2:3]
        ids[:, n * count : (n + 1) * count] = value.astype(jnp.int32)
    history = lax.broadcasted_iota(jnp.int32, scale.shape, 1) // 2 % 16
    factor = jnp.zeros(scale.shape, F32)
    for c in range(16):
        factor = jnp.where(history == c, temper[c], factor)
    scale[...] = factor
    top = jnp.full(scale.shape, -1e30, F32)
    total = jnp.zeros(scale.shape, F32)
    hit = jnp.zeros(scale.shape, F32)
    base = ids[...] - block_id[0] * items.shape[0]
    for part in tiles:
        logit = dot_nt(items[part], rows[...]) * scale[...]
        place = lax.broadcasted_iota(jnp.int32, logit.shape, 0)
        hit = hit + jnp.sum(jnp.where(place == base - part.start, logit, 0.0), axis=0, keepdims=True)
        new = jnp.maximum(top, jnp.max(logit, axis=0, keepdims=True))
        total = total * jnp.exp(top - new) + jnp.sum(jnp.exp(logit - new), axis=0, keepdims=True)
        top = new
    gap = jnp.zeros((5, count), F32)
    lines = []
    for n in range(2):
        lines += [v[:, n * count : (n + 1) * count] for v in (top, total, hit)] + [gap]
    lines = jnp.concatenate(lines + [jnp.zeros((112, count), F32)], axis=0)
    stats[...] = jnp.transpose(lines)[:, :16]


def loss_kernel(seen, loss):
    parts = []
    for n in (0, 8):
        top, total, hit = [seen[:, :, n + i : n + i + 1] for i in range(3)]
        peak = jnp.max(top, axis=0)
        whole = jnp.sum(total * jnp.exp(top - peak[None]), axis=0)
        parts.append(peak + jnp.log(whole) - jnp.sum(hit, axis=0))
    loss[...] = jnp.concatenate([p[k : k + 1] for p in parts for k in range(2)], axis=1)


def local(
    events, lengths, target_pos, target_ids, items, item_block, temper, in_gain, w_xbc, w_z, w_dt,
    conv_w, conv_b, dt_bias, a_log, d_skip, norm_gain, w_out, final_gain,
):
    rows, width = events.shape[1:]
    inner = w_z.shape[1]
    ev = events[0]
    spread = expander(32, 64, 2)
    chunks = rows // GROUP

    with jax.named_scope("halo"):
        halo = lax.ppermute(ev[rows - HALO :], SEQ, [(i, i + 1) for i in range(7)])

    with jax.named_scope("mix"):
        normed, cum, cum_t, shard, chunk, x, bc, keep, send = call(
            mix_kernel,
            [
                shape(rows, width), shape(rows, 128), shape(8, 4, rows, dtype=F32),
                shape(2, rows, 128), shape(3, rows, 128), shape(rows, inner), shape(rows, 256),
                shape(144, inner // 2), shape(144, inner // 2),
            ],
            [SMEM] + [HBM] * 10,
            [
                pltpu.VMEM((rows, width), BF), pltpu.VMEM((1, width), F32), pltpu.VMEM((32, width), BF),
                pltpu.VMEM((1, 32), F32), pltpu.VMEM((1, 32), F32), pltpu.VMEM((HALO, width), BF),
                pltpu.VMEM(w_xbc.shape, BF), pltpu.VMEM(conv_w.shape, F32),
                pltpu.VMEM((conv_b.shape[0] // 128, 128), F32), pltpu.VMEM(spread.shape, BF),
                pltpu.VMEM((rows + HALO, width), BF), pltpu.VMEM((rows, inner), BF),
                pltpu.VMEM((2, 2, rows + HALO, 128), F32),
                pltpu.VMEM((2, rows + 16, BLK), F32), pltpu.VMEM((2, rows, BLK), BF),
                pltpu.VMEM((128, rows), BF), pltpu.VMEM((144, inner), BF), pltpu.VMEM((rows + 16, 128), BF),
                pltpu.SemaphoreType.DMA((10,)), pltpu.SemaphoreType.DMA((9,)),
            ],
            2 * rows * width * 2304,
            limit=56,
            outs=[HBM] + [VMEM] * 4 + [HBM] + [VMEM] * 3,
        )(
            lengths, ev, in_gain[None], w_dt.T, dt_bias[None], a_log[None], halo, w_xbc, conv_w,
            conv_b.reshape(-1, 128), spread,
        )

    swap = [(0, 1), (1, 0)]
    payload = shape(144, inner // 2)
    entry = shape(128, inner // 2)
    with jax.named_scope("chip"):
        got = lax.ppermute(send, "core", swap)
        held = call(hold_kernel, payload, [VMEM])(keep)
        chip = call(chip_kernel, payload, [VMEM] * 2)(held, got)
        before = [
            lax.ppermute(chip, "x", [(i, i + n) for i in range(4 - n)]) for n in (1, 2, 3)
        ]
        x, chip = lax.optimization_barrier((x, chip))
    with jax.named_scope("scan"):
        y = call(
            scan_kernel,
            shape(rows, inner),
            [VMEM] * 6,
            [
                pltpu.VMEM((chunks, GROUP, GROUP), BF), pltpu.VMEM((128, rows), BF),
                pltpu.VMEM((rows + 16, 128), BF), pltpu.VMEM((128, BLK), jnp.int32),
                pltpu.VMEM((128, 4 * GROUP), jnp.int32), pltpu.VMEM((2, rows + 16, BLK), F32),
                pltpu.VMEM((2, rows, BLK), F32), pltpu.VMEM((2, rows, BLK), F32),
                pltpu.VMEM((2, rows, 4 * GROUP), F32),
            ],
            16 * rows * 128 * inner,
            limit=56,
        )(x, bc, cum, cum_t, chunk, d_skip[None])
        y, source = lax.optimization_barrier((y, normed))
    with jax.named_scope("gate"):
        z = dot(source, w_z).astype(BF)
        before, z = lax.optimization_barrier((before, z))
    with jax.named_scope("enter"):
        here, away = call(enter_kernel, [entry, entry], [VMEM] * 5)(keep, got, *before)
        there = lax.ppermute(away, "core", swap)

    with jax.named_scope("out"):
        out, picked = call(
            out_kernel,
            [shape(rows, width), shape(8, 4, width)],
            [VMEM] * 12,
            [
                pltpu.VMEM((rows, inner), BF), pltpu.VMEM((rows, 128), F32), pltpu.VMEM((128, inner), BF),
                pltpu.VMEM((rows, width), F32), pltpu.VMEM((rows, width), BF),
            ],
            2 * rows * inner * (width + 256),
            limit=14,
        )(
            y, bc, here, there, shard, z, ev, norm_gain[None], w_out, final_gain[None], target_pos,
            spread,
        )

    with jax.named_scope("rows"):
        mine = lax.all_to_all(picked, SEQ, 0, 0, tiled=True)
        sent = call(rows_kernel, shape(128, 2, width + 128), [SMEM, VMEM])(target_ids, mine)
        own_rows = lax.all_to_all(sent, EACH, 0, 0, tiled=True).reshape(256, width + 128)
        own_rows, source = lax.optimization_barrier((own_rows, items))
        got_rows = lax.ppermute(own_rows, "core", swap)
        items_v = call(hold_kernel, shape(*items.shape), [VMEM])(source)

    with jax.named_scope("logits"):
        stats = call(
            logit_kernel,
            shape(256, 16, dtype=F32),
            [SMEM, SMEM, VMEM, VMEM, VMEM],
            [
                pltpu.VMEM((512, width), BF), pltpu.VMEM((1, 512), jnp.int32), pltpu.VMEM((1, 512), F32),
            ],
            2 * 512 * items.shape[0] * width,
        )(item_block, temper, own_rows, got_rows, items_v)

    with jax.named_scope("loss"):
        seen = lax.all_to_all(stats.reshape(128, 2, 16), EACH, 0, 0, tiled=True)
        loss = call(loss_kernel, shape(1, 4, dtype=F32), [VMEM])(seen).reshape(4)
    return (out[None], loss)


def solution(mesh):
    fine = jax.sharding.Mesh(
        mesh.devices.reshape(mesh.shape["seq"] // 2, 2, mesh.shape["cand"]), ("x", "core", "cand")
    )
    each = ("x", "core", "cand")
    placed = (
        P("cand", SEQ, None),
        P("cand"),
        P("cand", None),
        P("cand", SEQ),
        P(each, None),
        P(each),
    ) + (P(),) * 13
    return jax.shard_map(
        local,
        mesh=fine,
        in_specs=placed,
        out_specs=(P("cand", SEQ, None), P(each)),
        check_vma=False,
    )
```

```python
import jax
import jax.numpy as jnp
import numpy as np
from jax import lax
from jax.experimental import pallas as pl
from jax.experimental.pallas import tpu as pltpu
from jax.sharding import PartitionSpec as P

GROUP = 128
EPS = 1e-05
BLK = 256
HALO = 16
PART = 64
LOG2E = 1.4426950408889634
BF = jnp.bfloat16
F32 = jnp.float32
SEQ = ("x", "core")
EACH = ("core", "x", "cand")
VMEM = pl.BlockSpec(memory_space=pltpu.VMEM)
HBM = pl.BlockSpec(memory_space=pl.ANY)
SMEM = pl.BlockSpec(memory_space=pltpu.SMEM)


def rms(v, gain):
    return v * lax.rsqrt(jnp.mean(v * v, axis=-1, keepdims=True) + EPS) * gain


def silu(v):
    half = 0.5 * v
    return half + half * jnp.tanh(half)


def four(v, axis=1):
    return jnp.concatenate([v, v, v, v], axis=axis)


def packed(v, parts):
    group = lax.broadcasted_iota(jnp.int32, v.shape, 1) // 32
    rest = v
    out = jnp.zeros_like(v)
    for part in range(parts):
        piece = rest.astype(BF).astype(F32)
        out = jnp.where(group == part, piece, out)
        rest = rest - piece
    return out.astype(BF)


def expander(heads, lanes, parts):
    row = np.arange(128)[:, None]
    col = np.arange(heads * lanes)[None, :]
    return jnp.asarray((row % 32 == col // lanes) & (row < 32 * parts), BF)


def dot(a, b):
    return jnp.dot(a, b, preferred_element_type=F32)


def dot_nt(a, b):
    return lax.dot_general(a, b, (((1,), (1,)), ((), ())), preferred_element_type=F32)


def blocks(total, size):
    return [slice(i, i + size) for i in range(0, total, size)]


def call(kernel, out_shape, specs, scratch=(), flops=0, limit=12, outs=None):
    many = isinstance(out_shape, (list, tuple))
    return pl.pallas_call(
        kernel,
        in_specs=specs,
        out_specs=outs or ([VMEM] * len(out_shape) if many else VMEM),
        out_shape=out_shape,
        scratch_shapes=list(scratch),
        compiler_params=pltpu.CompilerParams(vmem_limit_bytes=limit * 1024 * 1024),
        cost_estimate=pl.CostEstimate(flops=flops, bytes_accessed=0, transcendentals=0),
    )


def shape(*dims, dtype=BF):
    return jax.ShapeDtypeStruct(dims, dtype)


def fetches(pairs, sems, started=None):
    copies = [pltpu.make_async_copy(src, dst, sems.at[i]) for i, (src, dst) in enumerate(pairs)]
    for copy in copies[:started]:
        copy.start()
    return copies


def mix_kernel(
    length, ev_h, gain_h, w_dt_h, dt_bias_h, a_log_h, halo_h, w_h, conv_w_h, conv_b_h, spread_h,
    normed_h, cum_out, cum_t, shard, chunk, x_h, bc, keep, send,
    ev, gain, w_dt, dt_bias, a_log, halo, w, conv_w, conv_b, spread,
    full, x, raw, tail, weighted, b_t, states, fades, sems, out_sems,
):
    rows, inner = x.shape
    order = [slice(inner, inner + BLK)] + blocks(inner, BLK)
    copies = fetches(
        [
            (ev_h, ev), (gain_h, gain), (w_dt_h, w_dt), (dt_bias_h, dt_bias), (a_log_h, a_log),
            (halo_h, halo), (conv_w_h, conv_w), (conv_b_h, conv_b), (spread_h, spread), (w_h, w),
        ],
        sems,
    )
    for copy in copies[:6]:
        copy.wait()
    full[:HALO] = rms(halo[...].astype(F32), gain[...]).astype(BF)
    for part in blocks(rows, PART):
        full[HALO + part.start : HALO + part.stop] = rms(ev[part].astype(F32), gain[...]).astype(BF)
    pre = dot_nt(full[HALO:], four(w_dt[...], 0))
    place = lax.axis_index(SEQ) * rows + lax.broadcasted_iota(jnp.int32, (rows, 128), 0)
    v = pre + four(dt_bias[...])
    soft = jnp.maximum(v, 0.0) + jnp.log1p(jnp.exp(-jnp.abs(v)))
    step = jnp.where(place < length[0], soft, 0.0)
    logdec = -step * jnp.exp(four(a_log[...]))
    lower = (
        lax.broadcasted_iota(jnp.int32, (rows, rows), 0)
        >= lax.broadcasted_iota(jnp.int32, (rows, rows), 1)
    ).astype(BF)
    cum = dot(lower, packed(logdec, 3))
    cum = cum + pltpu.roll(cum, 32, 1)
    cum = cum + pltpu.roll(cum, 64, 1)
    scaled = cum * LOG2E
    cum_out[...] = packed(scaled, 3)
    flipped = jnp.transpose(scaled)
    for g in range(8):
        cum_t[g] = flipped[4 * g : 4 * g + 4]
    shard[0] = packed(jnp.exp(cum[rows - 1 :] - cum) * step, 2)
    shard[1] = packed(jnp.exp(cum), 2)
    chunk[0] = packed(step, 2)
    for c, part in enumerate(blocks(rows, GROUP)):
        own = cum[part]
        chunk[1, part] = packed(jnp.exp(own[GROUP - 1 :] - own) * step[part], 2)
        chunk[2, part] = packed(jnp.exp(own - (cum[part.start - 1 : part.start] if c else 0.0)), 2)
    for copy in copies[6:]:
        copy.wait()
    stores = [pltpu.make_async_copy(full.at[HALO:], normed_h, out_sems.at[2])]
    stores[0].start()
    fades[:rows] = shard[0]
    fades[rows:] = shard[1, rows - 16 :]

    def project(n):
        both = dot(full[...], w[:, order[n]])
        raw[n % 2, 0] = both[:, :128]
        raw[n % 2, 1] = both[:, 128:]
        if n:
            tail[n % 2] = dot(fades[...], spread[:, order[n]])

    def end_state(n):
        cols = order[n]
        states[:128, cols] = dot(b_t[...], weighted[n % 2]).astype(BF)
        states[128:, cols] = jnp.broadcast_to(tail[n % 2, rows + 15 :], (16, BLK)).astype(BF)

    project(0)
    for n, cols in enumerate(order):
        slot = n % 2
        if n + 1 < len(order):
            if n > 1:
                end_state(n - 1)
            project(n + 1)
        for j in range(2):
            at = cols.start // 128 + j
            lanes = slice(at * 128, (at + 1) * 128)
            local_lanes = slice(j * 128, (j + 1) * 128)
            for part in blocks(rows, PART):
                conv = conv_b[at : at + 1]
                for k in range(4):
                    first = HALO - 3 + k + part.start
                    conv = conv + conv_w[k : k + 1, lanes] * raw[slot, j, first : first + PART]
                act = silu(conv)
                if n:
                    x[part, lanes] = act.astype(BF)
                    weighted[slot, part, local_lanes] = (act * tail[slot, part, local_lanes]).astype(BF)
                else:
                    bc[part, local_lanes] = act.astype(BF)
        if n == 0:
            b_t[...] = jnp.transpose(bc[:, :128].astype(F32)).astype(BF)
        if n == 6:
            done = slice(0, cols.stop)
            stores += fetches([(x.at[:, done], x_h.at[:, done])], out_sems.at[0:1])
    rest = slice(order[6].stop, inner)
    stores += fetches([(x.at[:, rest], x_h.at[:, rest])], out_sems.at[1:2])
    end_state(len(order) - 2)
    end_state(len(order) - 1)
    first = lax.axis_index("core") == 0
    half = inner // 2
    for part in blocks(144, 48):
        low, high = states[part, :half], states[part, half:]
        keep[part] = jnp.where(first, low, high)
        send[part] = jnp.where(first, high, low)
    for store in stores:
        store.wait()


def join(first, second, out):
    decay = second[128:129].astype(F32)
    for part in blocks(128, PART):
        out[part] = (first[part].astype(F32) * decay + second[part].astype(F32)).astype(BF)
    out[128:] = (first[128:].astype(F32) * second[128:].astype(F32)).astype(BF)


def hold_kernel(keep, held):
    for part in blocks(keep.shape[0], 16):
        held[part] = keep[part]


def chip_kernel(keep, got, chip):
    @pl.when(lax.axis_index("core") == 0)
    def _():
        join(keep, got, chip)

    @pl.when(lax.axis_index("core") == 1)
    def _():
        join(got, keep, chip)


def enter_kernel(keep, got, near, mid, far, here, away):
    front = lax.axis_index("core") == 0
    near_decay, mid_decay = near[128:129].astype(F32), mid[128:129].astype(F32)
    decay = jnp.where(front, keep[128:129].astype(F32), got[128:129].astype(F32))
    for part in blocks(128, PART):
        enter = mid[part].astype(F32) + mid_decay * far[part].astype(F32)
        enter = near[part].astype(F32) + near_decay * enter
        first = jnp.where(front, keep[part].astype(F32), got[part].astype(F32))
        later = first + decay * enter
        here[part] = jnp.where(front, enter, later).astype(BF)
        away[part] = jnp.where(front, later, enter).astype(BF)


def head_offsets(lanes, heads, parts):
    row = lax.broadcasted_iota(jnp.int32, (128, heads * lanes), 0)
    col = lax.broadcasted_iota(jnp.int32, (128, heads * lanes), 1)
    return jnp.where(row < 32 * parts, (row & 31) - col // lanes, -1000)


def scan_kernel(
    x, bc, cum, cum_t, chunk, d_skip, y, scores, b_t, firsts, narrow, wide, steps, tails, insides, times
):
    rows, inner = x.shape
    narrow[...] = head_offsets(64, 4, 2)
    wide[...] = head_offsets(GROUP, 4, 3)
    lower = lax.broadcasted_iota(jnp.int32, (GROUP, GROUP), 0) >= lax.broadcasted_iota(
        jnp.int32, (GROUP, GROUP), 1
    )
    parts = blocks(rows, GROUP)
    for c, part in enumerate(parts):
        scores[c] = jnp.where(lower, dot_nt(bc[part, 128:], bc[part, :128]), 0.0).astype(BF)
    b_t[...] = jnp.transpose(bc[:, :128].astype(F32)).astype(BF)
    firsts[:rows] = chunk[0]
    firsts[rows:] = packed(jnp.broadcast_to(four(d_skip[...]), (16, 128)), 2)
    left = (lax.broadcasted_iota(jnp.int32, (GROUP, 128), 1) < 64).astype(F32).astype(BF)
    right = (lax.broadcasted_iota(jnp.int32, (GROUP, 128), 1) >= 64).astype(F32).astype(BF)

    def widen(g):
        slot = g % 2
        sp = (narrow[...] == 4 * g).astype(F32).astype(BF)
        wd = (wide[...] == 4 * g).astype(F32).astype(BF)
        steps[slot] = dot(firsts[...], sp)
        tails[slot] = dot(chunk[1], sp)
        insides[slot] = dot(chunk[2], sp)
        times[slot] = dot(cum[...], wd)

    def group(g):
        slot = g % 2
        cols = slice(g * BLK, (g + 1) * BLK)
        skip = steps[slot, rows : rows + 1]
        before = None
        entering = [None]
        for part in parts[:-1]:
            tailed = (x[part, cols].astype(F32) * tails[slot, part]).astype(BF)
            new = dot(b_t[:, part], tailed)
            before = new if before is None else before * insides[slot, part.stop - 1 : part.stop] + new
            entering.append(before.astype(BF))
        for c, part in enumerate(parts):
            xc = x[part, cols].astype(F32)
            stepped = (xc * steps[slot, part]).astype(BF)
            out = xc * skip
            if c:
                out = out + dot(bc[part, 128:], entering[c]) * insides[slot, part]
            pairs = []
            for p in range(2):
                weights = []
                for h in (2 * p, 2 * p + 1):
                    diff = times[slot, part, h * GROUP : (h + 1) * GROUP] - cum_t[g, h : h + 1, part]
                    weights.append(jnp.exp2(jnp.minimum(diff, 0.0)).astype(BF) * scores[c])
                pair = stepped[:, p * 128 : (p + 1) * 128]
                stacked = jnp.concatenate([pair * left, pair * right], axis=0)
                pairs.append(dot(jnp.concatenate(weights, axis=1), stacked))
            y[part, cols] = (out + jnp.concatenate(pairs, axis=1)).astype(BF)

    widen(0)
    for g in range(inner // BLK):
        if g + 1 < inner // BLK:
            widen(g + 1)
        group(g)


def out_kernel(
    y, bc, kept, got, shard, z, ev, norm_gain, w_out, final_gain, wanted, spread,
    out, picked, mixed, square, enter, total, final,
):
    rows, inner = z.shape
    width = ev.shape[1]
    half = inner // 2
    first = lax.axis_index("core") == 0
    enter[:, :half] = jnp.where(first, kept[...], got[...])
    enter[:, half:] = jnp.where(first, got[...], kept[...])
    tiles = blocks(inner, BLK)

    def spread_state(n):
        return dot(bc[:, 128:], enter[:, tiles[n]]), dot(shard[1], spread[:, tiles[n]])

    ahead = spread_state(0)
    for n, cols in enumerate(tiles):
        state, decay = ahead
        if n + 1 < len(tiles):
            ahead = spread_state(n + 1)
        for part in blocks(rows, PART):
            v = y[part, cols].astype(F32) + state[part] * decay[part]
            v = v * z[part, cols].astype(F32)
            sq = v * v
            sq = sq[:, :128] + sq[:, 128:]
            square[part] = square[part] + sq if n else sq
            mixed[part, cols] = (v * norm_gain[:, cols]).astype(BF)
    for cols in blocks(width, BLK):
        total[:, cols] = dot(mixed[...], w_out[:, cols])
    for part in blocks(rows, PART):
        mean = jnp.sum(square[part], axis=1, keepdims=True) * (1.0 / inner)
        res = (ev[part].astype(F32) + total[part] * lax.rsqrt(mean + EPS)).astype(BF)
        out[part] = res
        final[part] = rms(res.astype(F32), final_gain[...]).astype(BF)
    place = lax.axis_index(SEQ) * rows + lax.broadcasted_iota(jnp.int32, (32, rows), 1)
    column = jnp.transpose(jnp.broadcast_to(wanted[...].astype(F32), (128, 32)))[:, :1]
    pick = dot((place.astype(F32) == column).astype(BF), final[...]).astype(BF)
    for s in range(8):
        picked[s] = pick[4 * s : 4 * s + 4]


def rows_kernel(ids, got, sent):
    width = got.shape[2]
    mine = got[0].astype(F32)
    for s in range(1, got.shape[0]):
        mine = mine + got[s].astype(F32)
    row = lax.broadcasted_iota(jnp.int32, (4, 128), 0)
    lane = lax.broadcasted_iota(jnp.int32, (4, 128), 1)
    own = jnp.zeros((4, 128), jnp.int32)
    for k in range(4):
        own = jnp.where(row == k, ids[0, k], own)
    digits = jnp.where(lane == 0, own >> 16, jnp.where(lane == 1, (own >> 8) & 255, own & 255))
    digits = jnp.where(lane < 3, digits, 0).astype(F32)
    both = jnp.concatenate([mine, digits], axis=1).astype(BF)
    count = sent.shape[0] // 2
    for d in range(count):
        sent[d] = both[:2]
        sent[count + d] = both[2:]


def logit_kernel(block_id, temper, own, got, items, stats, rows, ids, scale):
    count, width = own.shape[0], items.shape[1]
    tiles = blocks(items.shape[0], 512)
    first = lax.axis_index("core") == 0
    for part in blocks(count, PART):
        mine, other = own[part], got[part]
        low = jnp.where(first, mine, other)
        high = jnp.where(first, other, mine)
        rows[part] = low[:, :width]
        rows[count + part.start : count + part.stop] = high[:, :width]
    for n in range(2):
        digits = jnp.where(first == (n == 0), own[:, width:], got[:, width:]).astype(F32)
        digits = jnp.transpose(digits)
        value = digits[0:1] * 65536.0 + digits[1:2] * 256.0 + digits[2:3]
        ids[:, n * count : (n + 1) * count] = value.astype(jnp.int32)
    history = lax.broadcasted_iota(jnp.int32, scale.shape, 1) // 2 % 16
    factor = jnp.zeros(scale.shape, F32)
    for c in range(16):
        factor = jnp.where(history == c, temper[c], factor)
    scale[...] = factor
    top = jnp.full(scale.shape, -1e30, F32)
    total = jnp.zeros(scale.shape, F32)
    hit = jnp.zeros(scale.shape, F32)
    base = ids[...] - block_id[0] * items.shape[0]
    for part in tiles:
        logit = dot_nt(items[part], rows[...]) * scale[...]
        place = lax.broadcasted_iota(jnp.int32, logit.shape, 0)
        hit = hit + jnp.sum(jnp.where(place == base - part.start, logit, 0.0), axis=0, keepdims=True)
        new = jnp.maximum(top, jnp.max(logit, axis=0, keepdims=True))
        total = total * jnp.exp(top - new) + jnp.sum(jnp.exp(logit - new), axis=0, keepdims=True)
        top = new
    gap = jnp.zeros((5, count), F32)
    lines = []
    for n in range(2):
        lines += [v[:, n * count : (n + 1) * count] for v in (top, total, hit)] + [gap]
    lines = jnp.concatenate(lines + [jnp.zeros((112, count), F32)], axis=0)
    stats[...] = jnp.transpose(lines)[:, :16]


def loss_kernel(seen, loss):
    parts = []
    for n in (0, 8):
        top, total, hit = [seen[:, :, n + i : n + i + 1] for i in range(3)]
        peak = jnp.max(top, axis=0)
        whole = jnp.sum(total * jnp.exp(top - peak[None]), axis=0)
        parts.append(peak + jnp.log(whole) - jnp.sum(hit, axis=0))
    loss[...] = jnp.concatenate([p[k : k + 1] for p in parts for k in range(2)], axis=1)


def local(
    events, lengths, target_pos, target_ids, items, item_block, temper, in_gain, w_xbc, w_z, w_dt,
    conv_w, conv_b, dt_bias, a_log, d_skip, norm_gain, w_out, final_gain,
):
    rows, width = events.shape[1:]
    inner = w_z.shape[1]
    ev = events[0]
    spread = expander(32, 64, 2)
    chunks = rows // GROUP

    with jax.named_scope("halo"):
        halo = lax.ppermute(ev[rows - HALO :], SEQ, [(i, i + 1) for i in range(7)])

    with jax.named_scope("mix"):
        normed, cum, cum_t, shard, chunk, x, bc, keep, send = call(
            mix_kernel,
            [
                shape(rows, width), shape(rows, 128), shape(8, 4, rows, dtype=F32),
                shape(2, rows, 128), shape(3, rows, 128), shape(rows, inner), shape(rows, 256),
                shape(144, inner // 2), shape(144, inner // 2),
            ],
            [SMEM] + [HBM] * 10,
            [
                pltpu.VMEM((rows, width), BF), pltpu.VMEM((1, width), F32), pltpu.VMEM((32, width), BF),
                pltpu.VMEM((1, 32), F32), pltpu.VMEM((1, 32), F32), pltpu.VMEM((HALO, width), BF),
                pltpu.VMEM(w_xbc.shape, BF), pltpu.VMEM(conv_w.shape, F32),
                pltpu.VMEM((conv_b.shape[0] // 128, 128), F32), pltpu.VMEM(spread.shape, BF),
                pltpu.VMEM((rows + HALO, width), BF), pltpu.VMEM((rows, inner), BF),
                pltpu.VMEM((2, 2, rows + HALO, 128), F32),
                pltpu.VMEM((2, rows + 16, BLK), F32), pltpu.VMEM((2, rows, BLK), BF),
                pltpu.VMEM((128, rows), BF), pltpu.VMEM((144, inner), BF), pltpu.VMEM((rows + 16, 128), BF),
                pltpu.SemaphoreType.DMA((10,)), pltpu.SemaphoreType.DMA((9,)),
            ],
            2 * rows * width * 2304,
            limit=56,
            outs=[HBM] + [VMEM] * 4 + [HBM] + [VMEM] * 3,
        )(
            lengths, ev, in_gain[None], w_dt.T, dt_bias[None], a_log[None], halo, w_xbc, conv_w,
            conv_b.reshape(-1, 128), spread,
        )

    swap = [(0, 1), (1, 0)]
    payload = shape(144, inner // 2)
    entry = shape(128, inner // 2)
    with jax.named_scope("chip"):
        got = lax.ppermute(send, "core", swap)
        held = call(hold_kernel, payload, [VMEM])(keep)
        chip = call(chip_kernel, payload, [VMEM] * 2)(held, got)
        before = [
            lax.ppermute(chip, "x", [(i, i + n) for i in range(4 - n)]) for n in (1, 2, 3)
        ]
        x, chip = lax.optimization_barrier((x, chip))
    with jax.named_scope("scan"):
        y = call(
            scan_kernel,
            shape(rows, inner),
            [VMEM] * 6,
            [
                pltpu.VMEM((chunks, GROUP, GROUP), BF), pltpu.VMEM((128, rows), BF),
                pltpu.VMEM((rows + 16, 128), BF), pltpu.VMEM((128, BLK), jnp.int32),
                pltpu.VMEM((128, 4 * GROUP), jnp.int32), pltpu.VMEM((2, rows + 16, BLK), F32),
                pltpu.VMEM((2, rows, BLK), F32), pltpu.VMEM((2, rows, BLK), F32),
                pltpu.VMEM((2, rows, 4 * GROUP), F32),
            ],
            16 * rows * 128 * inner,
            limit=56,
        )(x, bc, cum, cum_t, chunk, d_skip[None])
        y, source = lax.optimization_barrier((y, normed))
    with jax.named_scope("gate"):
        z = silu(dot(source, w_z).astype(BF).astype(F32)).astype(BF)
        before, z = lax.optimization_barrier((before, z))
    with jax.named_scope("enter"):
        here, away = call(enter_kernel, [entry, entry], [VMEM] * 5)(keep, got, *before)
        there = lax.ppermute(away, "core", swap)

    with jax.named_scope("out"):
        out, picked = call(
            out_kernel,
            [shape(rows, width), shape(8, 4, width)],
            [VMEM] * 12,
            [
                pltpu.VMEM((rows, inner), BF), pltpu.VMEM((rows, 128), F32), pltpu.VMEM((128, inner), BF),
                pltpu.VMEM((rows, width), F32), pltpu.VMEM((rows, width), BF),
            ],
            2 * rows * inner * (width + 256),
            limit=14,
        )(
            y, bc, here, there, shard, z, ev, norm_gain[None], w_out, final_gain[None], target_pos,
            spread,
        )

    with jax.named_scope("rows"):
        mine = lax.all_to_all(picked, SEQ, 0, 0, tiled=True)
        sent = call(rows_kernel, shape(128, 2, width + 128), [SMEM, VMEM])(target_ids, mine)
        own_rows = lax.all_to_all(sent, EACH, 0, 0, tiled=True).reshape(256, width + 128)
        own_rows, source = lax.optimization_barrier((own_rows, items))
        got_rows = lax.ppermute(own_rows, "core", swap)
        items_v = call(hold_kernel, shape(*items.shape), [VMEM])(source)

    with jax.named_scope("logits"):
        stats = call(
            logit_kernel,
            shape(256, 16, dtype=F32),
            [SMEM, SMEM, VMEM, VMEM, VMEM],
            [
                pltpu.VMEM((512, width), BF), pltpu.VMEM((1, 512), jnp.int32), pltpu.VMEM((1, 512), F32),
            ],
            2 * 512 * items.shape[0] * width,
        )(item_block, temper, own_rows, got_rows, items_v)

    with jax.named_scope("loss"):
        seen = lax.all_to_all(stats.reshape(128, 2, 16), EACH, 0, 0, tiled=True)
        loss = call(loss_kernel, shape(1, 4, dtype=F32), [VMEM])(seen).reshape(4)
    return (out[None], loss)


def solution(mesh):
    fine = jax.sharding.Mesh(
        mesh.devices.reshape(mesh.shape["seq"] // 2, 2, mesh.shape["cand"]), ("x", "core", "cand")
    )
    each = ("x", "core", "cand")
    placed = (
        P("cand", SEQ, None),
        P("cand"),
        P("cand", None),
        P("cand", SEQ),
        P(each, None),
        P(each),
    ) + (P(),) * 13
    return jax.shard_map(
        local,
        mesh=fine,
        in_specs=placed,
        out_specs=(P("cand", SEQ, None), P(each)),
        check_vma=False,
    )
```
